32 devices in a mesh: blk: 4 (over y, x), tile: 8 (over z, core).
Axes of the slice: x: 2, y: 2, z: 4, core: 2. Of those that a mesh axis runs over, the one named last changes fastest.
Arguments:
- left_rows: bfloat16 [1024, 49152], P('blk', 'tile'), may hold values from -0.1875 to 0.1875
- right_rows: bfloat16 [1024, 4096], P('blk', 'tile'), may hold values from -6 to 6
- row_weight: float32 [1024], P('blk'), may hold values from 0.25 to 4
- coupling: float32 [1024], P('blk'), may hold values from -6 to 6
- assign: int32 [8], replicated, may hold values from 0 to 3, as said below
- orders: int32 [8], replicated, may hold values from 42 to 214, as said below
- offsets: int32 [8], replicated, may hold values from 0 to 214, as said below
Outputs:
- schur_band: bfloat16 [4096, 49152], P('blk', 'tile')
The draws below stay inside these ranges and needn't reach their ends.
Inputs may be any that keep to these rules, and one draw needn't show every extreme that they name: `assign`: each blk index names exactly 2 blocks. The orders of the blocks that one blk index names sum to at most 256, and to exactly 256 for some index in every draw. offsets[b] is the sum of the orders of the blocks before b in the list that name the same blk index.
All inputs are finite; a program needn't handle non-finite values.
Results may differ from the reference program's by a relative error of at most 0.013.
Values may be sent and summed in bfloat16 or wider, within the bound.
No kernel may reach another device: no remote copies, remote signals or barrier semaphores. Data moves between devices by JAX's collectives and lax.ppermute only.
A program may use at most 128 MiB of HBM per device.

```python
import math
import jax
import jax.numpy as jnp
from jax import lax

DUAL = 49152
BAND = 4096
CAP = 256
BLK_DEV = 2
NBLOCKS = 8
ROWS = 1024
N_BLK = 4


def layout_draw(base_key):
    least_rows = CAP // 6
    key_first = jax.random.fold_in(base_key, 11)
    key_second = jax.random.fold_in(base_key, 12)
    key_third = jax.random.fold_in(base_key, 13)
    shuffled = jax.random.permutation(key_first, NBLOCKS)
    assign = (shuffled // BLK_DEV).astype(jnp.int32)
    block_ids = jnp.arange(NBLOCKS, dtype=jnp.int32)
    same_dev = assign[None, :] == assign[:, None]
    earlier = block_ids[None, :] < block_ids[:, None]
    before_count = jnp.sum((same_dev & earlier).astype(jnp.int32), axis=1)
    is_first = before_count == 0
    first_draw = jax.random.randint(key_second, (NBLOCKS,), least_rows, CAP - least_rows + 1, dtype=jnp.int32)
    first_draw = jnp.where(block_ids == 0, CAP - least_rows, first_draw).astype(jnp.int32)
    first_orders = jnp.where(is_first, first_draw, 0).astype(jnp.int32)
    partner_first = jnp.sum(jnp.where(same_dev & earlier, first_orders[None, :], 0), axis=1).astype(jnp.int32)
    raw_second = jax.random.randint(key_third, (NBLOCKS,), 0, 1048576, dtype=jnp.int32)
    second_span = CAP - partner_first - least_rows + 1
    second_orders = least_rows + raw_second % jnp.maximum(second_span, 1)
    orders = jnp.where(is_first, first_draw, second_orders).astype(jnp.int32)
    offsets = jnp.sum(jnp.where(same_dev & earlier, orders[None, :], 0), axis=1).astype(jnp.int32)
    return (assign, orders, offsets)


def draw_assign(key, part):
    return layout_draw(key)[0]


def draw_orders(key, part):
    return layout_draw(key)[1]


def draw_offsets(key, part):
    return layout_draw(key)[2]


def block_scale(own_key, shape, cuts, least, top_value):
    loudness, own = 1.0, jax.random.fold_in(own_key, 6)
    for dim, shards_of in cuts:
        steps = jnp.exp(jax.random.uniform(jax.random.fold_in(own, dim), (shards_of,), jnp.float32, least / len(cuts), top_value / len(cuts)))
        loudness = loudness * jnp.repeat(steps, shape[dim] // shards_of).reshape([-1 if axis == dim else 1 for axis in range(len(shape))])
    return loudness


def centred(key, dims, scale, most, shards=(), kind=jnp.bfloat16):
    result = scale * jax.random.normal(key, dims, jnp.float32)
    if shards:
        result = result * block_scale(key, dims, shards, -0.22, 0.18)
    return jnp.clip(result, -most, most).astype(kind)


def setup_inputs(seed: int = 0) -> dict:
    keys = jax.random.split(jax.random.key(seed), 8)
    left_rows = centred(keys[0], (ROWS, DUAL), (CAP * N_BLK) ** -0.5, 0.1875, ((0, 4), (1, 8)))
    right_rows = centred(keys[1], (ROWS, BAND), 1.0, 6.0, ((0, 4), (1, 8)))
    row_weight = jnp.clip(jnp.exp(math.log(4.0) - 2.7725887 * jax.random.uniform(keys[2], (ROWS,), jnp.float32) ** block_scale(keys[2], (ROWS,), ((0, 4),), -0.2, 0.2)), 0.25, 4.0)
    coupling = centred(keys[3], (ROWS,), 1.0, 6.0, ((0, 4),), jnp.float32)
    assign = draw_assign(jax.random.fold_in(keys[7], 71), 0)
    orders = draw_orders(jax.random.fold_in(keys[7], 71), 0)
    offsets = draw_offsets(jax.random.fold_in(keys[7], 71), 0)
    return {"left_rows": left_rows, "right_rows": right_rows, "row_weight": row_weight, "coupling": coupling, "assign": assign, "orders": orders, "offsets": offsets}


def reference(left_rows, right_rows, row_weight, coupling, assign, orders, offsets):
    total_rows = left_rows.shape[0]
    height = total_rows // N_BLK
    row_index = jnp.arange(total_rows, dtype=jnp.int32)
    owner_dev = row_index // height
    local_row = row_index % height
    member = ((owner_dev[:, None] == assign[None, :]) & (local_row[:, None] >= offsets[None, :]) & (local_row[:, None] < offsets[None, :] + orders[None, :])).astype(jnp.float32)
    is_live = lax.optimization_barrier(jnp.sum(member, axis=1, keepdims=True))
    right_wide = right_rows.astype(jnp.float32)
    block_sums = jnp.dot(member.T, coupling[:, None] * right_wide, precision=lax.Precision.HIGHEST)
    block_terms = block_sums / jnp.sqrt(orders.astype(jnp.float32))[:, None]
    spread_back = jnp.dot(member, block_terms, precision=lax.Precision.HIGHEST)
    weighted = (is_live * row_weight[:, None] * right_wide + coupling[:, None] * spread_back).astype(jnp.bfloat16)
    left_slabs = left_rows.reshape(N_BLK, height, left_rows.shape[1])
    weighted_slabs = weighted.reshape(N_BLK, height, weighted.shape[1])

    def add_slab(running, slab_pair):
        slab_term = lax.dot_general(slab_pair[1], slab_pair[0], (((0,), (0,)), ((), ())), preferred_element_type=jnp.float32)
        slab_term = lax.optimization_barrier(slab_term.astype(jnp.bfloat16)).astype(jnp.float32)
        return (running + slab_term, None)
    running, _ = lax.scan(add_slab, jnp.zeros((BAND, DUAL), jnp.float32), (left_slabs, weighted_slabs))
    return running.astype(jnp.bfloat16)
```

```python
import jax
import jax.numpy as jnp
from jax import lax
from jax.experimental import pallas as pl
from jax.experimental.pallas import tpu as pltpu
from jax.sharding import PartitionSpec as P

UNITS = 12
CHUNKS = (2, 4, 5, 1)


def weigh_rows(right_rows, row_weight, coupling, member, orders):
    right_wide = right_rows.astype(jnp.float32)
    block_sums = jnp.dot(member.T, coupling[:, None] * right_wide, precision=lax.Precision.HIGHEST)
    block_terms = block_sums / jnp.sqrt(orders.astype(jnp.float32))[:, None]
    spread_back = jnp.dot(member, block_terms, precision=lax.Precision.HIGHEST)
    is_live = jnp.sum(member, axis=1, keepdims=True)
    return (is_live * row_weight[:, None] * right_wide + coupling[:, None] * spread_back).astype(
        jnp.bfloat16
    )


def on_ring(place, count):
    half = count // 2
    return jnp.where(place < half, place, count + half - 1 - place)


def ring_shift(count, by):
    half = count // 2
    ring = list(range(half)) + list(range(count - 1, half - 1, -1))
    return [(ring[p], ring[(p + by) % count]) for p in range(count)]


def exchange_weighted(weighted):
    blks, tiles = lax.axis_size("blk"), lax.axis_size("tile")
    ring_place = on_ring(lax.axis_index("blk"), blks)
    rows = lax.all_to_all(weighted, "tile", split_axis=0, concat_axis=1, tiled=True)
    width = rows.shape[1] // blks
    parts = []
    for step in range(blks):
        target = on_ring(lax.rem(ring_place + step, blks), blks)
        part = lax.dynamic_slice_in_dim(rows, target * width, width, 1)
        parts.append(lax.ppermute(part, "blk", ring_shift(blks, step)) if step else part)
    held = jnp.stack(parts)
    axis, bit = 0, tiles // 2
    while bit:
        other = lax.ppermute(held, "tile", [(t, t ^ bit) for t in range(tiles)])
        upper = (lax.axis_index("tile") & bit) != 0
        held = jnp.stack(
            [jnp.where(upper, other, held), jnp.where(upper, held, other)], axis=axis
        )
        axis, bit = axis + 1, bit // 2
    held = held.reshape((tiles, blks, rows.shape[0], width))
    return held.transpose((3, 1, 0, 2)).reshape((width, blks * weighted.shape[0]))


def gather_left(piece):
    blks = lax.axis_size("blk")
    forth, back = ring_shift(blks, 1), ring_shift(blks, -1)
    low, high = [piece], [piece]
    for _ in range(blks // 2 - 1):
        low.append(lax.ppermute(low[-1], "blk", forth))
        high.append(lax.ppermute(high[-1], "blk", back))
    half = piece.shape[0] // 2
    far = [lax.ppermute(low[-1][:half], "blk", forth), lax.ppermute(high[-1][half:], "blk", back)]
    return low[1:] + far + high[:0:-1]


def band_kernel(*refs):
    weights, pieces, out = refs[0], refs[1:-1], refs[-1]
    stacked = jnp.concatenate([piece[...] for piece in pieces], axis=0)
    out[...] = jnp.dot(weights[...], stacked, preferred_element_type=jnp.float32).astype(out.dtype)


def band_kernel_onto(*refs):
    band_kernel(*refs[1:])


def band_chunk(band, weights, left_rows, others, first, unit):
    height, columns = left_rows.shape
    width = others[0].shape[1]
    rows, depth = weights.shape
    here = lambda j: (0, first + j)
    specs = [pl.BlockSpec((rows, depth), lambda j: (0, 0)), pl.BlockSpec((height, unit), here)]
    specs += [pl.BlockSpec((o.shape[0], unit), lambda j: (0, j)) for o in others]
    operands = [weights, left_rows, *others]
    kernel, aliases = band_kernel, {}
    if band is not None:
        specs.insert(0, pl.BlockSpec(memory_space=pl.ANY))
        operands.insert(0, band)
        kernel, aliases = band_kernel_onto, {0: 0}
    return pl.pallas_call(
        kernel,
        grid=(width // unit,),
        in_specs=specs,
        out_specs=pl.BlockSpec((rows, unit), here),
        out_shape=jax.ShapeDtypeStruct((rows, columns), jnp.bfloat16),
        input_output_aliases=aliases,
        compiler_params=pltpu.CompilerParams(vmem_limit_bytes=32 * 1024 * 1024),
        cost_estimate=pl.CostEstimate(
            flops=2 * rows * depth * width,
            bytes_accessed=2 * (rows * depth + depth * width + rows * width),
            transcendentals=0,
        ),
    )(*operands)


def shards(left_rows, right_rows, row_weight, coupling, assign, orders, offsets):
    height, columns = left_rows.shape
    my_index = lax.axis_index("blk")
    unit = columns // UNITS
    gathered, start = [], 0
    for size in CHUNKS:
        piece = left_rows[:, start * unit : (start + size) * unit]
        gathered.append((start, gather_left(piece)))
        start += size

    row_ids = lax.broadcasted_iota(jnp.int32, (height, assign.shape[0]), 0)
    member = (
        (assign[None, :] == my_index)
        & (row_ids >= offsets[None, :])
        & (row_ids < offsets[None, :] + orders[None, :])
    ).astype(jnp.float32)
    weighted = weigh_rows(right_rows, row_weight, coupling, member, orders)
    weights = exchange_weighted(weighted)

    band = None
    for start, others in gathered:
        band = band_chunk(band, weights, left_rows, others, start, unit)
    return band


def solution(mesh):
    return jax.shard_map(
        shards,
        mesh=mesh,
        in_specs=(P("blk", "tile"), P("blk", "tile"), P("blk"), P("blk"), P(), P(), P()),
        out_specs=P("blk", "tile"),
        check_vma=False,
    )
```

```python
import functools

import jax
import jax.numpy as jnp
from jax import lax
from jax.experimental import pallas as pl
from jax.experimental.pallas import tpu as pltpu
from jax.sharding import PartitionSpec as P

UNITS = 24
SENDS = ((8,), (6, 4, 4, 2))
LANES = 128
VMEM_LIMIT = 20 * 1024 * 1024
VMEM_MOST = 60 * 1024 * 1024


def cost(weight):
    return pl.CostEstimate(flops=weight * 10**6, bytes_accessed=0, transcendentals=0)


def on_ring(place, count):
    half = count // 2
    return jnp.where(place < half, place, count + half - 1 - place)


def ring_shift(count, by):
    half = count // 2
    ring = list(range(half)) + list(range(count - 1, half - 1, -1))
    return [(ring[p], ring[(p + by) % count]) for p in range(count)]


def block_width(first, size, unit):
    return 2 * unit if first % (2 * unit) == 0 and size % (2 * unit) == 0 else unit


def swap(count, distance):
    return [(t, t ^ distance) for t in range(count)]


def my_group():
    members = lax.axis_size("tile") // lax.axis_size("blk")
    return lax.axis_index("tile") // members


def token_spec():
    return pl.BlockSpec((16, LANES), lambda i: (0, 0))


def token_shape():
    return jax.ShapeDtypeStruct((16, LANES), jnp.bfloat16)


def as_columns(row, width):
    column = jnp.broadcast_to(row, (LANES, row.shape[1])).T
    return jnp.concatenate([column] * (width // LANES), axis=1)


def weigh_kernel(groups, *refs):
    sources, outs = refs[:6], refs[7 : 7 + groups]
    *held, weighted, sems = refs[7 + groups :]
    copies = [
        pltpu.make_async_copy(source, target, sems.at[i])
        for i, (source, target) in enumerate(zip(sources, held))
    ]
    for copy in copies:
        copy.start()
    for copy in copies:
        copy.wait()
    assign, orders, offsets, right, row_weight, coupling = held
    height, width = right.shape
    me = lax.axis_index("blk")
    right_wide = right[...].astype(jnp.float32)
    coupled = as_columns(coupling[...], width)
    scaled = coupled * right_wide
    row_ids = lax.broadcasted_iota(jnp.int32, (height, width), 0)
    live = jnp.zeros((height, width), jnp.float32)
    spread = jnp.zeros((height, width), jnp.float32)
    for b in range(assign.shape[0]):
        mine = assign[b] == me
        first = jnp.where(mine, offsets[b], 0)
        last = jnp.where(mine, offsets[b] + orders[b], 0)
        member = ((row_ids >= first) & (row_ids < last)).astype(jnp.float32)
        block_sum = jnp.sum(member * scaled, axis=0, keepdims=True)
        root = jnp.sqrt(jnp.full((1, width), orders[b], jnp.int32).astype(jnp.float32))
        spread += member * (block_sum / root)
        live += member
    result = live * as_columns(row_weight[...], width) * right_wide + coupled * spread
    weighted[...] = result.astype(jnp.bfloat16)
    group, rows = my_group(), outs[0].shape[0]
    for distance, out in enumerate(outs):
        start = pl.multiple_of(jnp.bitwise_xor(group, distance) * rows, rows)
        out[...] = weighted[pl.ds(start, rows), :]


def weigh_rows(right_rows, row_weight, coupling, assign, orders, offsets, after):
    height, width = right_rows.shape
    groups = lax.axis_size("blk")
    row_weight, coupling = row_weight.reshape(1, height), coupling.reshape(1, height)
    operands = (assign, orders, offsets, right_rows, row_weight, coupling)
    spaces = [pltpu.SMEM] * 3 + [pltpu.VMEM] * 3
    return pl.pallas_call(
        functools.partial(weigh_kernel, groups),
        grid=(1,),
        in_specs=[pl.BlockSpec(memory_space=pl.ANY)] * 6 + [token_spec()],
        out_specs=[pl.BlockSpec((height // groups, width), lambda i: (0, 0))] * groups,
        out_shape=[jax.ShapeDtypeStruct((height // groups, width), jnp.bfloat16)] * groups,
        scratch_shapes=[space(a.shape, a.dtype) for space, a in zip(spaces, operands)]
        + [pltpu.VMEM((height, width), jnp.bfloat16), pltpu.SemaphoreType.DMA((6,))],
        compiler_params=pltpu.CompilerParams(vmem_limit_bytes=VMEM_MOST),
        cost_estimate=cost(100000),
    )(*operands, after)


def pick_kernel(*refs):
    count = (len(refs) - 2) // 2
    pieces, outs, token, held = refs[:count], refs[count:-2], refs[-2], refs[-1]
    token[...] = jnp.zeros_like(token)
    for distance, piece in enumerate(pieces):
        held[distance] = piece[...]
    place = on_ring(lax.axis_index("blk"), count)
    group = my_group()
    for step, out in enumerate(outs):
        target = on_ring(lax.rem(place + step, count), count)
        out[...] = held[jnp.bitwise_xor(group, target)]


def pick_columns(pieces):
    count = len(pieces)
    return pl.pallas_call(
        pick_kernel,
        out_shape=[jax.ShapeDtypeStruct(pieces[0].shape, pieces[0].dtype)] * count
        + [token_shape()],
        scratch_shapes=[pltpu.VMEM((count, *pieces[0].shape), pieces[0].dtype)],
        compiler_params=pltpu.CompilerParams(vmem_limit_bytes=VMEM_LIMIT),
        cost_estimate=cost(1),
    )(*pieces)


def stack_kernel(*refs):
    parts, (_, out, token) = refs[:-3], refs[-3:]
    token[...] = jnp.zeros_like(token)
    for step, part in enumerate(parts):
        out[step] = part[...]


def whole_spec(shape):
    return pl.BlockSpec(tuple(shape), lambda i: (0,) * len(shape))


def stack_parts(parts, after, weight=1):
    shape = (len(parts), *parts[0].shape)
    return pl.pallas_call(
        stack_kernel,
        grid=(1,),
        in_specs=[whole_spec(part.shape) for part in parts] + [token_spec()],
        out_specs=[whole_spec(shape), token_spec()],
        out_shape=[jax.ShapeDtypeStruct(shape, parts[0].dtype), token_shape()],
        compiler_params=pltpu.CompilerParams(vmem_limit_bytes=VMEM_LIMIT),
        cost_estimate=cost(weight),
    )(*parts, after)


def arrange_kernel(far_groups, *refs):
    pieces, (_, out, token, held) = refs[:-4], refs[-4:]
    token[...] = jnp.zeros_like(token)
    _, slabs, rows, width = pieces[0].shape
    height = held.shape[0] // slabs
    group, member = my_group(), lax.rem(lax.axis_index("tile"), len(pieces))
    for far_member, piece in enumerate(pieces):
        column = pl.multiple_of(jnp.bitwise_xor(member, far_member) * width, width)
        for index, far_group in enumerate(far_groups):
            row = pl.multiple_of(jnp.bitwise_xor(group, far_group) * rows, rows)
            for slab in range(slabs):
                held[pl.ds(slab * height + row, rows), pl.ds(column, width)] = piece[index, slab]
    for slab in range(slabs):
        part = pl.ds(slab * height, height)
        out[:, part] = held[part, :].T


def arrange(pieces, far_groups, height, after):
    _, slabs, _, width = pieces[0].shape
    shape = (len(pieces) * width, slabs * height)
    return pl.pallas_call(
        functools.partial(arrange_kernel, far_groups),
        grid=(1,),
        in_specs=[whole_spec(piece.shape) for piece in pieces] + [token_spec()],
        out_specs=[whole_spec(shape), token_spec()],
        out_shape=[jax.ShapeDtypeStruct(shape, jnp.bfloat16), token_shape()],
        scratch_shapes=[pltpu.VMEM(shape[::-1], jnp.bfloat16)],
        compiler_params=pltpu.CompilerParams(vmem_limit_bytes=VMEM_LIMIT),
        cost_estimate=cost(1),
    )(*pieces, after)


def slice_kernel(left, *refs):
    out, token = refs[-2:]
    out[...] = left[...]
    token[...] = jnp.zeros_like(token)


def slice_columns(left_rows, first, size, unit, after):
    unit = block_width(first, size, unit)
    height, begin = left_rows.shape[0], first // unit
    return pl.pallas_call(
        slice_kernel,
        grid=(size // unit,),
        in_specs=[pl.BlockSpec((height, unit), lambda j: (0, begin + j))]
        + [token_spec()] * len(after),
        out_specs=[pl.BlockSpec((height, unit), lambda j: (0, j)), token_spec()],
        out_shape=[jax.ShapeDtypeStruct((height, size), left_rows.dtype), token_shape()],
        compiler_params=pltpu.CompilerParams(vmem_limit_bytes=VMEM_LIMIT),
        cost_estimate=cost(1),
    )(left_rows, *after)


def send_slab(piece):
    blks = lax.axis_size("blk")
    forth, back = ring_shift(blks, 1), ring_shift(blks, -1)
    ahead, behind = [], []
    for _ in range(blks // 2 - 1):
        ahead.append(lax.ppermute(ahead[-1] if ahead else piece, "blk", forth))
        behind.append(lax.ppermute(behind[-1] if behind else piece, "blk", back))
    return ahead, behind


def cut_kernel(ahead, behind, *refs):
    low, high, token = refs[-3:]
    low[...] = ahead[...]
    high[...] = behind[...]
    token[...] = jnp.zeros_like(token)


def cut_far(ahead, behind, first, size, unit, after):
    half = ahead[-1].shape[0] // 2
    unit = size if first % size == 0 else block_width(first, size, unit)
    begin = first // unit
    out_spec = pl.BlockSpec((half, unit), lambda j: (0, j))
    return pl.pallas_call(
        cut_kernel,
        grid=(size // unit,),
        in_specs=[
            pl.BlockSpec((half, unit), lambda j: (0, begin + j)),
            pl.BlockSpec((half, unit), lambda j: (1, begin + j)),
        ]
        + [token_spec()] * len(after),
        out_specs=[out_spec] * 2 + [token_spec()],
        out_shape=[jax.ShapeDtypeStruct((half, size), ahead[-1].dtype)] * 2 + [token_shape()],
        compiler_params=pltpu.CompilerParams(vmem_limit_bytes=VMEM_LIMIT),
        cost_estimate=cost(1),
    )(ahead[-1], behind[-1], *after)


def send_far(cuts):
    blks = lax.axis_size("blk")
    return [lax.ppermute(cut, "blk", ring_shift(blks, by)) for cut, by in zip(cuts, (1, -1))]


def band_kernel(*refs):
    weights, pieces, (_, out, token) = refs[0], refs[1:-3], refs[-3:]
    token[...] = jnp.zeros_like(token)
    stacked = jnp.concatenate([piece[...] for piece in pieces], axis=0)
    out[...] = jnp.dot(weights[...], stacked, preferred_element_type=jnp.float32).astype(out.dtype)


def band_kernel_onto(*refs):
    band_kernel(*refs[1:])


def band_chunk(band, weights, pieces, width, columns, unit, after):
    rows, depth = weights.shape

    def spec(array, first):
        return pl.BlockSpec((array.shape[0], unit), lambda j: (0, first // unit + j))

    specs = [pl.BlockSpec((rows, depth), lambda j: (0, 0))]
    specs += [spec(array, first) for array, first in pieces]
    specs.append(token_spec())
    operands = [weights] + [array for array, _ in pieces] + [after]
    kernel, aliases = band_kernel, {}
    if band is not None:
        specs.insert(0, pl.BlockSpec(memory_space=pl.ANY))
        operands.insert(0, band)
        kernel, aliases = band_kernel_onto, {0: 0}
    begin = pieces[0][1] // unit
    return pl.pallas_call(
        kernel,
        grid=(width // unit,),
        in_specs=specs,
        out_specs=[pl.BlockSpec((rows, unit), lambda j: (0, begin + j)), token_spec()],
        out_shape=[
            jax.ShapeDtypeStruct((rows, columns), jnp.bfloat16),
            token_shape(),
        ],
        input_output_aliases=aliases,
        compiler_params=pltpu.CompilerParams(vmem_limit_bytes=VMEM_LIMIT),
        cost_estimate=cost(1),
    )(*operands)


def shards(left_rows, right_rows, row_weight, coupling, assign, orders, offsets):
    height, columns = left_rows.shape
    blks, tiles = lax.axis_size("blk"), lax.axis_size("tile")
    members = tiles // blks
    unit = columns // UNITS

    starts = [sum(map(sum, SENDS[:i])) * unit for i in range(len(SENDS))]
    widths = [sum(sizes) * unit for sizes in SENDS]
    head = left_rows[:, : widths[0]]
    streams = [send_slab(head)]

    blocks = weigh_rows(right_rows, row_weight, coupling, assign, orders, offsets, head)
    pieces = [blocks[0]]
    for distance in range(1, blks):
        pieces.append(lax.ppermute(blocks[distance], "tile", swap(tiles, distance * members)))
    *parts, token = pick_columns(pieces)
    for step in range(1, blks):
        parts[step] = lax.ppermute(parts[step], "blk", ring_shift(blks, step))

    chunks = []

    def send_chunk(which, place, token, after=()):
        (ahead, behind), width = streams[which], SENDS[which][place] * unit
        offset = sum(SENDS[which][:place]) * unit
        *cuts, token = cut_far(ahead, behind, offset, width, unit, [token, *after])
        chunks.append((starts[which] + offset, offset, width, ahead, behind, send_far(cuts)))
        return token

    def send_slice(which, token, after=()):
        slab, token = slice_columns(left_rows, starts[which], widths[which], unit, [token, *after])
        streams.append(send_slab(slab))
        return token

    def multiply(band, index, token):
        begin, offset, width, ahead, behind, far = chunks[index]
        pieces = (
            [(left_rows, begin)]
            + [(array, offset) for array in ahead]
            + [(array, 0) for array in far]
            + [(array, offset) for array in behind[::-1]]
        )
        block = block_width(begin, width, unit)
        return band_chunk(band, weights, pieces, width, columns, block, token)

    token = send_slice(1, token)
    token = send_chunk(0, 0, token)
    held, token = stack_parts(parts, token, 100000)
    held, far_groups = held[None], [0]
    bit = blks // 2
    while bit:
        moved = lax.ppermute(held, "tile", swap(tiles, bit * members))
        held, token = stack_parts([held, moved], token)
        held = held.reshape((-1, *held.shape[2:]))
        far_groups = far_groups + [group ^ bit for group in far_groups]
        bit //= 2
    by_member = {0: held}
    bit = members // 2
    while bit:
        for member, piece in list(by_member.items()):
            by_member[member ^ bit] = lax.ppermute(piece, "tile", swap(tiles, bit))
        bit //= 2
    pieces = [by_member[member] for member in range(members)]
    weights, token = arrange(pieces, far_groups, height, token)

    band = None
    token = send_chunk(1, 0, token)
    for index in range(len(SENDS[1]) + 1):
        if index + 1 < len(SENDS[1]):
            token = send_chunk(1, index + 1, token, chunks[index][-1])
        band, token = multiply(band, index, token)
    return band


def solution(mesh):
    return jax.shard_map(
        shards,
        mesh=mesh,
        in_specs=(P("blk", "tile"), P("blk", "tile"), P("blk"), P("blk"), P(), P(), P()),
        out_specs=P("blk", "tile"),
        check_vma=False,
    )
```

```python
import functools

import jax
import jax.numpy as jnp
from jax import lax
from jax.experimental import pallas as pl
from jax.experimental.pallas import tpu as pltpu
from jax.sharding import PartitionSpec as P

UNITS = 24
SENDS = ((8,), (6, 7), (3,))
SHIFT = (0, 16, 0, 0)
LANES = 128
VMEM_LIMIT = 20 * 1024 * 1024


def cost(weight):
    return pl.CostEstimate(flops=weight * 10**6, bytes_accessed=0, transcendentals=0)


def on_ring(place, count):
    half = count // 2
    return jnp.where(place < half, place, count + half - 1 - place)


def ring_shift(count, by):
    half = count // 2
    ring = list(range(half)) + list(range(count - 1, half - 1, -1))
    return [(ring[p], ring[(p + by) % count]) for p in range(count)]


def block_width(first, size, unit):
    return 2 * unit if first % (2 * unit) == 0 and size % (2 * unit) == 0 else unit


def swap(count, distance):
    return [(t, t ^ distance) for t in range(count)]


def my_group():
    members = lax.axis_size("tile") // lax.axis_size("blk")
    return lax.axis_index("tile") // members


def token_spec():
    return pl.BlockSpec((16, LANES), lambda i: (0, 0))


def token_shape():
    return jax.ShapeDtypeStruct((16, LANES), jnp.bfloat16)


def as_columns(row, width):
    column = jnp.broadcast_to(row, (LANES, row.shape[1])).T
    return jnp.concatenate([column] * (width // LANES), axis=1)


def weigh_kernel(groups, *refs):
    sources, outs = refs[:6], refs[7 : 7 + groups]
    *held, weighted, sems = refs[7 + groups :]
    copies = [
        pltpu.make_async_copy(source, target, sems.at[i])
        for i, (source, target) in enumerate(zip(sources, held))
    ]
    for copy in copies:
        copy.start()
    for copy in copies:
        copy.wait()
    assign, orders, offsets, right, row_weight, coupling = held
    height, width = right.shape
    me = lax.axis_index("blk")
    right_wide = right[...].astype(jnp.float32)
    coupled = as_columns(coupling[...], width)
    scaled = coupled * right_wide
    row_ids = lax.broadcasted_iota(jnp.int32, (height, width), 0)
    live = jnp.zeros((height, width), jnp.float32)
    spread = jnp.zeros((height, width), jnp.float32)
    for b in range(assign.shape[0]):
        mine = assign[b] == me
        first = jnp.where(mine, offsets[b], 0)
        last = jnp.where(mine, offsets[b] + orders[b], 0)
        member = ((row_ids >= first) & (row_ids < last)).astype(jnp.float32)
        block_sum = jnp.sum(member * scaled, axis=0, keepdims=True)
        root = jnp.sqrt(jnp.full((1, width), orders[b], jnp.int32).astype(jnp.float32))
        spread += member * (block_sum / root)
        live += member
    result = live * as_columns(row_weight[...], width) * right_wide + coupled * spread
    weighted[...] = result.astype(jnp.bfloat16)
    group, rows = my_group(), outs[0].shape[0]
    for distance, out in enumerate(outs):
        start = pl.multiple_of(jnp.bitwise_xor(group, distance) * rows, rows)
        out[...] = weighted[pl.ds(start, rows), :]


def weigh_rows(right_rows, row_weight, coupling, assign, orders, offsets, after):
    height, width = right_rows.shape
    groups = lax.axis_size("blk")
    row_weight, coupling = row_weight.reshape(1, height), coupling.reshape(1, height)
    operands = (assign, orders, offsets, right_rows, row_weight, coupling)
    spaces = [pltpu.SMEM] * 3 + [pltpu.VMEM] * 3
    return pl.pallas_call(
        functools.partial(weigh_kernel, groups),
        grid=(1,),
        in_specs=[pl.BlockSpec(memory_space=pltpu.HBM)] * 6 + [token_spec()],
        out_specs=[pl.BlockSpec((height // groups, width), lambda i: (0, 0))] * groups,
        out_shape=[jax.ShapeDtypeStruct((height // groups, width), jnp.bfloat16)] * groups,
        scratch_shapes=[space(a.shape, a.dtype) for space, a in zip(spaces, operands)]
        + [pltpu.VMEM((height, width), jnp.bfloat16), pltpu.SemaphoreType.DMA((6,))],
        compiler_params=pltpu.CompilerParams(vmem_limit_bytes=VMEM_LIMIT),
        cost_estimate=cost(100000),
    )(*operands, after)


def pick_kernel(*refs):
    count = (len(refs) - 2) // 2
    pieces, outs, token, held = refs[:count], refs[count:-2], refs[-2], refs[-1]
    token[...] = jnp.zeros_like(token)
    for distance, piece in enumerate(pieces):
        held[distance] = piece[...]
    place = on_ring(lax.axis_index("blk"), count)
    group = my_group()
    for step, out in enumerate(outs):
        target = on_ring(lax.rem(place + step, count), count)
        out[...] = held[jnp.bitwise_xor(group, target)]


def pick_columns(pieces):
    count = len(pieces)
    return pl.pallas_call(
        pick_kernel,
        out_shape=[jax.ShapeDtypeStruct(pieces[0].shape, pieces[0].dtype)] * count
        + [token_shape()],
        scratch_shapes=[pltpu.VMEM((count, *pieces[0].shape), pieces[0].dtype)],
        compiler_params=pltpu.CompilerParams(vmem_limit_bytes=VMEM_LIMIT),
        cost_estimate=cost(1),
    )(*pieces)


def stack_kernel(*refs):
    parts, (_, out, token) = refs[:-3], refs[-3:]
    token[...] = jnp.zeros_like(token)
    for step, part in enumerate(parts):
        out[step] = part[...]


def whole_spec(shape):
    return pl.BlockSpec(tuple(shape), lambda i: (0,) * len(shape))


def stack_parts(parts, after, weight=1):
    shape = (len(parts), *parts[0].shape)
    return pl.pallas_call(
        stack_kernel,
        grid=(1,),
        in_specs=[whole_spec(part.shape) for part in parts] + [token_spec()],
        out_specs=[whole_spec(shape), token_spec()],
        out_shape=[jax.ShapeDtypeStruct(shape, parts[0].dtype), token_shape()],
        compiler_params=pltpu.CompilerParams(vmem_limit_bytes=VMEM_LIMIT),
        cost_estimate=cost(weight),
    )(*parts, after)


def arrange_kernel(places, members, *refs):
    pieces, (_, out, token, held) = refs[:-4], refs[-4:]
    token[...] = jnp.zeros_like(token)
    _, slabs, rows, width = pieces[0].shape
    height = held.shape[0] // slabs
    group, member = my_group(), lax.rem(lax.axis_index("tile"), members)
    for (far_member, far_groups), piece in zip(places, pieces):
        column = pl.multiple_of(jnp.bitwise_xor(member, far_member) * width, width)
        for index, far_group in enumerate(far_groups):
            row = pl.multiple_of(jnp.bitwise_xor(group, far_group) * rows, rows)
            for slab in range(slabs):
                held[pl.ds(slab * height + row, rows), pl.ds(column, width)] = piece[index, slab]
    for place, slab in enumerate(sorted(range(slabs), key=lambda s: (s == slabs // 2, s))):
        out[:, pl.ds(place * height, height)] = held[pl.ds(slab * height, height), :].T


def arrange(places, pieces, members, height, after):
    _, slabs, _, width = pieces[0].shape
    shape = (members * width, slabs * height)
    return pl.pallas_call(
        functools.partial(arrange_kernel, places, members),
        grid=(1,),
        in_specs=[whole_spec(piece.shape) for piece in pieces] + [token_spec()],
        out_specs=[whole_spec(shape), token_spec()],
        out_shape=[jax.ShapeDtypeStruct(shape, jnp.bfloat16), token_shape()],
        scratch_shapes=[pltpu.VMEM(shape[::-1], jnp.bfloat16)],
        compiler_params=pltpu.CompilerParams(vmem_limit_bytes=VMEM_LIMIT),
        cost_estimate=cost(1),
    )(*pieces, after)


def slice_kernel(left, *refs):
    out, token = refs[-2:]
    out[...] = left[...]
    token[...] = jnp.zeros_like(token)


def slice_columns(left_rows, first, size, unit, after):
    unit = block_width(first, size, unit)
    height, begin = left_rows.shape[0], first // unit
    return pl.pallas_call(
        slice_kernel,
        grid=(size // unit,),
        in_specs=[pl.BlockSpec((height, unit), lambda j: (0, begin + j))]
        + [token_spec()] * len(after),
        out_specs=[pl.BlockSpec((height, unit), lambda j: (0, j)), token_spec()],
        out_shape=[jax.ShapeDtypeStruct((height, size), left_rows.dtype), token_shape()],
        compiler_params=pltpu.CompilerParams(vmem_limit_bytes=VMEM_LIMIT),
        cost_estimate=cost(1),
    )(left_rows, *after)


def send_slab(piece):
    blks = lax.axis_size("blk")
    forth, back = ring_shift(blks, 1), ring_shift(blks, -1)
    ahead, behind = [], []
    for _ in range(blks // 2 - 1):
        ahead.append(lax.ppermute(ahead[-1] if ahead else piece, "blk", forth))
        behind.append(lax.ppermute(behind[-1] if behind else piece, "blk", back))
    return ahead, behind


def cut_kernel(ahead, behind, *refs):
    low, high, token = refs[-3:]
    low[...] = ahead[: low.shape[0], :]
    high[...] = behind[low.shape[0] :, :]
    token[...] = jnp.zeros_like(token)


def cut_far(ahead, behind, first, size, unit, shift, after):
    unit = size if first % size == 0 else block_width(first, size, unit)
    height, begin = ahead[-1].shape[0], first // unit
    low, high = height // 2 - shift, height // 2 + shift
    return pl.pallas_call(
        cut_kernel,
        grid=(size // unit,),
        in_specs=[pl.BlockSpec((height, unit), lambda j: (0, begin + j))] * 2
        + [token_spec()] * len(after),
        out_specs=[
            pl.BlockSpec((low, unit), lambda j: (0, j)),
            pl.BlockSpec((high, unit), lambda j: (0, j)),
            token_spec(),
        ],
        out_shape=[
            jax.ShapeDtypeStruct((low, size), ahead[-1].dtype),
            jax.ShapeDtypeStruct((high, size), ahead[-1].dtype),
            token_shape(),
        ],
        compiler_params=pltpu.CompilerParams(vmem_limit_bytes=VMEM_LIMIT),
        cost_estimate=cost(1),
    )(ahead[-1], behind[-1], *after)


def send_far(cuts):
    blks = lax.axis_size("blk")
    return [lax.ppermute(cut, "blk", ring_shift(blks, by)) for cut, by in zip(cuts, (1, -1))]


def stacked_dot(weights, pieces):
    stacked = jnp.concatenate([piece[...] for piece in pieces], axis=0)
    return jnp.dot(weights, stacked, preferred_element_type=jnp.float32)


def near_kernel(*refs):
    weights, pieces, (_, out, token) = refs[0], refs[1:-3], refs[-3:]
    token[...] = jnp.zeros_like(token)
    depth = sum(piece.shape[0] for piece in pieces)
    out[...] = stacked_dot(weights[:, :depth], pieces)


def far_kernel_onto(_, *refs):
    far_kernel(*refs)


def far_kernel(near, weights, *refs):
    pieces, (_, out, token) = refs[:-3], refs[-3:]
    token[...] = jnp.zeros_like(token)
    rows, width = out.shape
    step = pl.program_id(0)
    if rows < near.shape[0]:
        here = near[pl.ds(pl.multiple_of(step * rows, rows), rows), :]
    else:
        here = near[:, pl.ds(pl.multiple_of(step * width, width), width)]
    out[...] = (here + stacked_dot(weights[...], pieces)).astype(out.dtype)


def piece_specs(pieces, unit):
    return [
        pl.BlockSpec((array.shape[0], unit), lambda j, begin=first // unit: (0, begin + j))
        for array, first in pieces
    ]


def near_chunk(weights, pieces, width, unit, after):
    rows, depth = weights.shape
    return pl.pallas_call(
        near_kernel,
        grid=(width // unit,),
        in_specs=[pl.BlockSpec((rows, depth), lambda j: (0, 0))]
        + piece_specs(pieces, unit)
        + [token_spec()],
        out_specs=[pl.BlockSpec((rows, unit), lambda j: (0, j)), token_spec()],
        out_shape=[jax.ShapeDtypeStruct((rows, width), jnp.float32), token_shape()],
        compiler_params=pltpu.CompilerParams(vmem_limit_bytes=VMEM_LIMIT),
        cost_estimate=cost(1),
    )(weights, *[array for array, _ in pieces], after)


def band_chunk(band, near, weights, pieces, begin, columns, unit, after):
    rows, width = near.shape
    slab = sum(piece.shape[0] for piece in pieces)
    last = weights.shape[1] // slab - 1
    kernel, operands, specs, aliases = far_kernel, [], [], {}
    if band is not None:
        kernel, operands, aliases = far_kernel_onto, [band], {0: 0}
        specs = [pl.BlockSpec(memory_space=pl.ANY)]
    specs.append(pl.BlockSpec(memory_space=pltpu.VMEM))
    if begin % width == 0:
        steps, place = 2, begin // width
        specs.append(pl.BlockSpec((rows // steps, slab), lambda i: (i, last)))
        specs += [whole_spec(piece.shape) for piece in pieces]
        out_spec = pl.BlockSpec((rows // steps, width), lambda i: (i, place))
    else:
        block = block_width(begin, width, unit)
        steps, place = width // block, begin // block
        specs.append(pl.BlockSpec((rows, slab), lambda i: (0, last)))
        specs += piece_specs([(piece, 0) for piece in pieces], block)
        out_spec = pl.BlockSpec((rows, block), lambda i: (0, place + i))
    return pl.pallas_call(
        kernel,
        grid=(steps,),
        in_specs=specs + [token_spec()],
        out_specs=[out_spec, token_spec()],
        out_shape=[jax.ShapeDtypeStruct((rows, columns), jnp.bfloat16), token_shape()],
        input_output_aliases=aliases,
        compiler_params=pltpu.CompilerParams(vmem_limit_bytes=VMEM_LIMIT),
        cost_estimate=cost(1),
    )(*operands, near, weights, *pieces, after)


def shards(left_rows, right_rows, row_weight, coupling, assign, orders, offsets):
    height, columns = left_rows.shape
    blks, tiles = lax.axis_size("blk"), lax.axis_size("tile")
    members = tiles // blks
    unit = columns // UNITS

    starts = [sum(map(sum, SENDS[:i])) * unit for i in range(len(SENDS))]
    widths = [sum(sizes) * unit for sizes in SENDS]
    head = left_rows[:, : widths[0]]
    streams = [send_slab(head)]

    blocks = weigh_rows(right_rows, row_weight, coupling, assign, orders, offsets, head)
    pieces = [blocks[0]]
    for distance in range(1, blks):
        pieces.append(lax.ppermute(blocks[distance], "tile", swap(tiles, distance * members)))
    *parts, token = pick_columns(pieces)
    for step in range(1, blks):
        parts[step] = lax.ppermute(parts[step], "blk", ring_shift(blks, step))

    chunks = []

    def send_chunk(which, place, token, after=()):
        (ahead, behind), width = streams[which], SENDS[which][place] * unit
        offset = sum(SENDS[which][:place]) * unit
        *cuts, token = cut_far(
            ahead, behind, offset, width, unit, SHIFT[len(chunks)], [token, *after]
        )
        chunks.append((starts[which] + offset, send_far(cuts)))
        return token

    def send_slice(which, token, after=()):
        slab, token = slice_columns(left_rows, starts[which], widths[which], unit, [token, *after])
        streams.append(send_slab(slab))
        return token

    def multiply_near(which, place, token):
        (ahead, behind), offset = streams[which], sum(SENDS[which][:place]) * unit
        width, begin = SENDS[which][place] * unit, starts[which] + offset
        pieces = [(left_rows, begin)] + [(array, offset) for array in ahead + behind[::-1]]
        return near_chunk(weights, pieces, width, block_width(begin, width, unit), token)

    def multiply(band, near, index, token):
        begin, far = chunks[index]
        return band_chunk(band, near, weights, far, begin, columns, unit, token)

    token = send_slice(1, token)
    token = send_chunk(0, 0, token)
    held, token = stack_parts(parts, token, 100000)
    held, far_groups = held[None], [0]
    bit = blks // 2
    while bit > 1:
        moved = lax.ppermute(held, "tile", swap(tiles, bit * members))
        held, token = stack_parts([held, moved], token)
        held = held.reshape((-1, *held.shape[2:]))
        far_groups = far_groups + [group ^ bit for group in far_groups]
        bit //= 2
    moved = lax.ppermute(held, "tile", swap(tiles, members))
    arrived = {(0, tuple(far_groups)): held, (0, tuple(g ^ 1 for g in far_groups)): moved}
    bit = members // 2
    while bit:
        for (member, groups), piece in list(arrived.items()):
            arrived[member ^ bit, groups] = lax.ppermute(piece, "tile", swap(tiles, bit))
        bit //= 2
    weights, token = arrange(
        list(arrived.keys()), list(arrived.values()), members, height, token
    )

    nears = [None] * sum(map(len, SENDS))
    nears[0], token = multiply_near(0, 0, token)
    token = send_slice(2, token, [streams[1][0][-1], streams[1][1][-1]])
    nears[1], token = multiply_near(1, 0, token)
    nears[2], token = multiply_near(1, 1, token)
    token = send_chunk(1, 0, token, chunks[0][-1])
    band, token = multiply(None, nears[0], 0, token)
    token = send_chunk(1, 1, token, [streams[2][0][-1], streams[2][1][-1]])
    nears[3], token = multiply_near(2, 0, token)
    token = send_chunk(2, 0, token, chunks[1][-1])
    for index in range(1, len(chunks)):
        band, token = multiply(band, nears[index], index, token)
    return band


def solution(mesh):
    return jax.shard_map(
        shards,
        mesh=mesh,
        in_specs=(P("blk", "tile"), P("blk", "tile"), P("blk"), P("blk"), P(), P(), P()),
        out_specs=P("blk", "tile"),
        check_vma=False,
    )
```

```python
import functools

import jax
import jax.numpy as jnp
from jax import lax
from jax.experimental import pallas as pl
from jax.experimental.pallas import tpu as pltpu
from jax.sharding import PartitionSpec as P

UNITS = 24
SENDS = ((8,), (6, 6), (4,))
SHIFT = (0, 16, 0, 0)
LANES = 128
VMEM_LIMIT = 16 * 1024 * 1024


def cost(weight):
    return pl.CostEstimate(flops=weight * 10**6, bytes_accessed=0, transcendentals=0)


def on_ring(place, count):
    half = count // 2
    return jnp.where(place < half, place, count + half - 1 - place)


def ring_shift(count, by):
    half = count // 2
    ring = list(range(half)) + list(range(count - 1, half - 1, -1))
    return [(ring[p], ring[(p + by) % count]) for p in range(count)]


def block_width(first, size, unit):
    return 2 * unit if first % (2 * unit) == 0 and size % (2 * unit) == 0 else unit


def swap(count, distance):
    return [(t, t ^ distance) for t in range(count)]


def my_group():
    members = lax.axis_size("tile") // lax.axis_size("blk")
    return lax.axis_index("tile") // members


def token_spec():
    return pl.BlockSpec((16, LANES), lambda i: (0, 0))


def token_shape():
    return jax.ShapeDtypeStruct((16, LANES), jnp.bfloat16)


def as_columns(row, width):
    column = jnp.broadcast_to(row, (LANES, row.shape[1])).T
    return jnp.concatenate([column] * (width // LANES), axis=1)


def weigh_kernel(groups, *refs):
    sources, outs = refs[:6], refs[7 : 7 + groups]
    *held, weighted, sems = refs[7 + groups :]
    copies = [
        pltpu.make_async_copy(source, target, sems.at[i])
        for i, (source, target) in enumerate(zip(sources, held))
    ]
    for copy in copies:
        copy.start()
    for copy in copies:
        copy.wait()
    assign, orders, offsets, right, row_weight, coupling = held
    height, width = right.shape
    me = lax.axis_index("blk")
    right_wide = right[...].astype(jnp.float32)
    coupled = as_columns(coupling[...], width)
    scaled = coupled * right_wide
    row_ids = lax.broadcasted_iota(jnp.int32, (height, width), 0)
    live = jnp.zeros((height, width), jnp.float32)
    spread = jnp.zeros((height, width), jnp.float32)
    for b in range(assign.shape[0]):
        mine = assign[b] == me
        first = jnp.where(mine, offsets[b], 0)
        last = jnp.where(mine, offsets[b] + orders[b], 0)
        member = ((row_ids >= first) & (row_ids < last)).astype(jnp.float32)
        block_sum = jnp.sum(member * scaled, axis=0, keepdims=True)
        root = jnp.sqrt(jnp.full((1, width), orders[b], jnp.int32).astype(jnp.float32))
        spread += member * (block_sum / root)
        live += member
    result = live * as_columns(row_weight[...], width) * right_wide + coupled * spread
    weighted[...] = result.astype(jnp.bfloat16)
    group, rows = my_group(), outs[0].shape[0]
    for distance, out in enumerate(outs):
        start = pl.multiple_of(jnp.bitwise_xor(group, distance) * rows, rows)
        out[...] = weighted[pl.ds(start, rows), :]


def weigh_rows(right_rows, row_weight, coupling, assign, orders, offsets, after):
    height, width = right_rows.shape
    groups = lax.axis_size("blk")
    row_weight, coupling = row_weight.reshape(1, height), coupling.reshape(1, height)
    operands = (assign, orders, offsets, right_rows, row_weight, coupling)
    spaces = [pltpu.SMEM] * 3 + [pltpu.VMEM] * 3
    return pl.pallas_call(
        functools.partial(weigh_kernel, groups),
        grid=(1,),
        in_specs=[pl.BlockSpec(memory_space=pltpu.HBM)] * 6 + [token_spec()],
        out_specs=[pl.BlockSpec((height // groups, width), lambda i: (0, 0))] * groups,
        out_shape=[jax.ShapeDtypeStruct((height // groups, width), jnp.bfloat16)] * groups,
        scratch_shapes=[space(a.shape, a.dtype) for space, a in zip(spaces, operands)]
        + [pltpu.VMEM((height, width), jnp.bfloat16), pltpu.SemaphoreType.DMA((6,))],
        compiler_params=pltpu.CompilerParams(vmem_limit_bytes=VMEM_LIMIT),
        cost_estimate=cost(100000),
    )(*operands, after)


def pick_kernel(*refs):
    count = (len(refs) - 2) // 2
    pieces, outs, token, held = refs[:count], refs[count:-2], refs[-2], refs[-1]
    token[...] = jnp.zeros_like(token)
    for distance, piece in enumerate(pieces):
        held[distance] = piece[...]
    place = on_ring(lax.axis_index("blk"), count)
    group = my_group()
    for step, out in enumerate(outs):
        target = on_ring(lax.rem(place + step, count), count)
        out[...] = held[jnp.bitwise_xor(group, target)]


def pick_columns(pieces):
    count = len(pieces)
    return pl.pallas_call(
        pick_kernel,
        out_shape=[jax.ShapeDtypeStruct(pieces[0].shape, pieces[0].dtype)] * count
        + [token_shape()],
        scratch_shapes=[pltpu.VMEM((count, *pieces[0].shape), pieces[0].dtype)],
        compiler_params=pltpu.CompilerParams(vmem_limit_bytes=VMEM_LIMIT),
        cost_estimate=cost(1),
    )(*pieces)


def stack_kernel(*refs):
    parts, (_, out, token) = refs[:-3], refs[-3:]
    token[...] = jnp.zeros_like(token)
    for step, part in enumerate(parts):
        out[step] = part[...]


def whole_spec(shape):
    return pl.BlockSpec(tuple(shape), lambda i: (0,) * len(shape))


def stack_parts(parts, after, weight=1):
    shape = (len(parts), *parts[0].shape)
    return pl.pallas_call(
        stack_kernel,
        grid=(1,),
        in_specs=[whole_spec(part.shape) for part in parts] + [token_spec()],
        out_specs=[whole_spec(shape), token_spec()],
        out_shape=[jax.ShapeDtypeStruct(shape, parts[0].dtype), token_shape()],
        compiler_params=pltpu.CompilerParams(vmem_limit_bytes=VMEM_LIMIT),
        cost_estimate=cost(weight),
    )(*parts, after)


def arrange_kernel(places, members, *refs):
    pieces, (_, out, token, held) = refs[:-4], refs[-4:]
    token[...] = jnp.zeros_like(token)
    _, slabs, rows, width = pieces[0].shape
    height = held.shape[0] // slabs
    group, member = my_group(), lax.rem(lax.axis_index("tile"), members)
    for (far_member, far_groups), piece in zip(places, pieces):
        column = pl.multiple_of(jnp.bitwise_xor(member, far_member) * width, width)
        for index, far_group in enumerate(far_groups):
            row = pl.multiple_of(jnp.bitwise_xor(group, far_group) * rows, rows)
            for slab in range(slabs):
                held[pl.ds(slab * height + row, rows), pl.ds(column, width)] = piece[index, slab]
    for place, slab in enumerate(sorted(range(slabs), key=lambda s: (s == slabs // 2, s))):
        out[:, pl.ds(place * height, height)] = held[pl.ds(slab * height, height), :].T


def arrange(places, pieces, members, height, after):
    _, slabs, _, width = pieces[0].shape
    shape = (members * width, slabs * height)
    return pl.pallas_call(
        functools.partial(arrange_kernel, places, members),
        grid=(1,),
        in_specs=[whole_spec(piece.shape) for piece in pieces] + [token_spec()],
        out_specs=[whole_spec(shape), token_spec()],
        out_shape=[jax.ShapeDtypeStruct(shape, jnp.bfloat16), token_shape()],
        scratch_shapes=[pltpu.VMEM(shape[::-1], jnp.bfloat16)],
        compiler_params=pltpu.CompilerParams(vmem_limit_bytes=VMEM_LIMIT),
        cost_estimate=cost(1),
    )(*pieces, after)


def slice_kernel(left, *refs):
    out, token = refs[-2:]
    out[...] = left[...]
    token[...] = jnp.zeros_like(token)


def slice_columns(left_rows, first, size, unit, after):
    unit = block_width(first, size, unit)
    height, begin = left_rows.shape[0], first // unit
    return pl.pallas_call(
        slice_kernel,
        grid=(size // unit,),
        in_specs=[pl.BlockSpec((height, unit), lambda j: (0, begin + j))]
        + [token_spec()] * len(after),
        out_specs=[pl.BlockSpec((height, unit), lambda j: (0, j)), token_spec()],
        out_shape=[jax.ShapeDtypeStruct((height, size), left_rows.dtype), token_shape()],
        compiler_params=pltpu.CompilerParams(vmem_limit_bytes=VMEM_LIMIT),
        cost_estimate=cost(1),
    )(left_rows, *after)


def send_slab(piece):
    blks = lax.axis_size("blk")
    forth, back = ring_shift(blks, 1), ring_shift(blks, -1)
    ahead, behind = [], []
    for _ in range(blks // 2 - 1):
        ahead.append(lax.ppermute(ahead[-1] if ahead else piece, "blk", forth))
        behind.append(lax.ppermute(behind[-1] if behind else piece, "blk", back))
    return ahead, behind


def cut_kernel(ahead, behind, *refs):
    low, high, token = refs[-3:]
    low[...] = ahead[: low.shape[0], :]
    high[...] = behind[low.shape[0] :, :]
    token[...] = jnp.zeros_like(token)


def cut_far(ahead, behind, first, size, unit, shift, after):
    unit = size if first % size == 0 else block_width(first, size, unit)
    height, begin = ahead[-1].shape[0], first // unit
    low, high = height // 2 - shift, height // 2 + shift
    return pl.pallas_call(
        cut_kernel,
        grid=(size // unit,),
        in_specs=[pl.BlockSpec((height, unit), lambda j: (0, begin + j))] * 2
        + [token_spec()] * len(after),
        out_specs=[
            pl.BlockSpec((low, unit), lambda j: (0, j)),
            pl.BlockSpec((high, unit), lambda j: (0, j)),
            token_spec(),
        ],
        out_shape=[
            jax.ShapeDtypeStruct((low, size), ahead[-1].dtype),
            jax.ShapeDtypeStruct((high, size), ahead[-1].dtype),
            token_shape(),
        ],
        compiler_params=pltpu.CompilerParams(vmem_limit_bytes=VMEM_LIMIT),
        cost_estimate=cost(1),
    )(ahead[-1], behind[-1], *after)


def send_far(cuts):
    blks = lax.axis_size("blk")
    return [lax.ppermute(cut, "blk", ring_shift(blks, by)) for cut, by in zip(cuts, (1, -1))]


def stacked_dot(weights, pieces):
    stacked = jnp.concatenate([piece[...] for piece in pieces], axis=0)
    return jnp.dot(weights, stacked, preferred_element_type=jnp.float32)


def near_kernel(*refs):
    weights, pieces, (_, out, token) = refs[0], refs[1:-3], refs[-3:]
    token[...] = jnp.zeros_like(token)
    depth = sum(piece.shape[0] for piece in pieces)
    out[...] = stacked_dot(weights[:, :depth], pieces)


def far_kernel_onto(_, *refs):
    far_kernel(*refs)


def far_kernel(near, weights, *refs):
    pieces, (_, out, token) = refs[:-3], refs[-3:]
    token[...] = jnp.zeros_like(token)
    rows, width = out.shape
    step = pl.program_id(0)
    stacked = jnp.concatenate([piece[...] for piece in pieces], axis=0)
    last = pl.ds(weights.shape[1] - stacked.shape[0], stacked.shape[0])
    if rows < near.shape[0]:
        down, across = pl.ds(pl.multiple_of(step * rows, rows), rows), slice(None)
    else:
        down, across = slice(None), pl.ds(pl.multiple_of(step * width, width), width)
    added = jnp.dot(weights[down, last], stacked, preferred_element_type=jnp.float32)
    out[...] = (near[down, across] + added).astype(out.dtype)


def piece_specs(pieces, unit):
    return [
        pl.BlockSpec((array.shape[0], unit), lambda j, begin=first // unit: (0, begin + j))
        for array, first in pieces
    ]


def near_chunk(weights, pieces, width, unit, after):
    rows, depth = weights.shape
    return pl.pallas_call(
        near_kernel,
        grid=(width // unit,),
        in_specs=[pl.BlockSpec((rows, depth), lambda j: (0, 0))]
        + piece_specs(pieces, unit)
        + [token_spec()],
        out_specs=[pl.BlockSpec((rows, unit), lambda j: (0, j)), token_spec()],
        out_shape=[jax.ShapeDtypeStruct((rows, width), jnp.float32), token_shape()],
        compiler_params=pltpu.CompilerParams(vmem_limit_bytes=VMEM_LIMIT),
        cost_estimate=cost(1),
    )(weights, *[array for array, _ in pieces], after)


def band_chunk(band, near, weights, pieces, begin, columns, unit, after):
    rows, width = near.shape
    kernel, operands, specs, aliases = far_kernel, [], [], {}
    if band is not None:
        kernel, operands, aliases = far_kernel_onto, [band], {0: 0}
        specs = [pl.BlockSpec(memory_space=pl.ANY)]
    specs += [pl.BlockSpec(memory_space=pltpu.VMEM)] * 2
    if begin % width == 0:
        steps, place = 2, begin // width
        specs += [pl.BlockSpec(memory_space=pltpu.VMEM)] * len(pieces)
        out_spec = pl.BlockSpec((rows // steps, width), lambda i: (i, place))
    else:
        block = block_width(begin, width, unit)
        steps, place = width // block, begin // block
        specs += piece_specs([(piece, 0) for piece in pieces], block)
        out_spec = pl.BlockSpec((rows, block), lambda i: (0, place + i))
    return pl.pallas_call(
        kernel,
        grid=(steps,),
        in_specs=specs + [token_spec()],
        out_specs=[out_spec, token_spec()],
        out_shape=[jax.ShapeDtypeStruct((rows, columns), jnp.bfloat16), token_shape()],
        input_output_aliases=aliases,
        compiler_params=pltpu.CompilerParams(vmem_limit_bytes=VMEM_LIMIT),
        cost_estimate=cost(1),
    )(*operands, near, weights, *pieces, after)


def shards(left_rows, right_rows, row_weight, coupling, assign, orders, offsets):
    height, columns = left_rows.shape
    blks, tiles = lax.axis_size("blk"), lax.axis_size("tile")
    members = tiles // blks
    unit = columns // UNITS

    starts = [sum(map(sum, SENDS[:i])) * unit for i in range(len(SENDS))]
    widths = [sum(sizes) * unit for sizes in SENDS]
    head = left_rows[:, : widths[0]]
    streams = [send_slab(head)]

    blocks = weigh_rows(right_rows, row_weight, coupling, assign, orders, offsets, head)
    pieces = [blocks[0]]
    for distance in range(1, blks):
        pieces.append(lax.ppermute(blocks[distance], "tile", swap(tiles, distance * members)))
    *parts, token = pick_columns(pieces)
    for step in range(1, blks):
        parts[step] = lax.ppermute(parts[step], "blk", ring_shift(blks, step))

    chunks = []

    def send_chunk(which, place, token, after=()):
        (ahead, behind), width = streams[which], SENDS[which][place] * unit
        offset = sum(SENDS[which][:place]) * unit
        *cuts, token = cut_far(
            ahead, behind, offset, width, unit, SHIFT[len(chunks)], [token, *after]
        )
        chunks.append((starts[which] + offset, send_far(cuts)))
        return token

    def send_slice(which, token, after=()):
        slab, token = slice_columns(left_rows, starts[which], widths[which], unit, [token, *after])
        streams.append(send_slab(slab))
        return token

    def multiply_near(which, place, token):
        (ahead, behind), offset = streams[which], sum(SENDS[which][:place]) * unit
        width, begin = SENDS[which][place] * unit, starts[which] + offset
        pieces = [(left_rows, begin)] + [(array, offset) for array in ahead + behind[::-1]]
        return near_chunk(weights, pieces, width, block_width(begin, width, unit), token)

    def multiply(band, near, index, token):
        begin, far = chunks[index]
        return band_chunk(band, near, weights, far, begin, columns, unit, token)

    token = send_slice(1, token)
    token = send_chunk(0, 0, token)
    held, token = stack_parts(parts, token, 100000)
    held, far_groups = held[None], [0]
    bit = blks // 2
    while bit > 1:
        moved = lax.ppermute(held, "tile", swap(tiles, bit * members))
        held, token = stack_parts([held, moved], token)
        held = held.reshape((-1, *held.shape[2:]))
        far_groups = far_groups + [group ^ bit for group in far_groups]
        bit //= 2
    moved = lax.ppermute(held, "tile", swap(tiles, members))
    arrived = {(0, tuple(far_groups)): held, (0, tuple(g ^ 1 for g in far_groups)): moved}
    bit = members // 2
    while bit:
        for (member, groups), piece in list(arrived.items()):
            arrived[member ^ bit, groups] = lax.ppermute(piece, "tile", swap(tiles, bit))
        bit //= 2
    weights, token = arrange(
        list(arrived.keys()), list(arrived.values()), members, height, token
    )

    nears = [None] * sum(map(len, SENDS))
    nears[0], token = multiply_near(0, 0, token)
    token = send_slice(2, token, [streams[1][0][-1], streams[1][1][-1]])
    nears[1], token = multiply_near(1, 0, token)
    nears[2], token = multiply_near(1, 1, token)
    token = send_chunk(1, 0, token, chunks[0][-1])
    band, token = multiply(None, nears[0], 0, token)
    token = send_chunk(1, 1, token, [streams[2][0][-1], streams[2][1][-1]])
    nears[3], token = multiply_near(2, 0, token)
    token = send_chunk(2, 0, token, chunks[1][-1])
    for index in range(1, len(chunks)):
        band, token = multiply(band, nears[index], index, token)
    return band


def solution(mesh):
    return jax.shard_map(
        shards,
        mesh=mesh,
        in_specs=(P("blk", "tile"), P("blk", "tile"), P("blk"), P("blk"), P(), P(), P()),
        out_specs=P("blk", "tile"),
        check_vma=False,
    )
```

```python
import functools

import jax
import jax.numpy as jnp
from jax import lax
from jax.experimental import pallas as pl
from jax.experimental.pallas import tpu as pltpu
from jax.sharding import PartitionSpec as P

UNITS = 24
SENDS = ((8,), (6, 6), (4,))
SHIFT = (0, 16, 0, 0)
LANES = 128
VMEM_LIMIT = 16 * 1024 * 1024


def cost(weight):
    return pl.CostEstimate(flops=weight * 10**6, bytes_accessed=0, transcendentals=0)


def on_ring(place, count):
    half = count // 2
    return jnp.where(place < half, place, count + half - 1 - place)


def ring_shift(count, by):
    half = count // 2
    ring = list(range(half)) + list(range(count - 1, half - 1, -1))
    return [(ring[p], ring[(p + by) % count]) for p in range(count)]


def block_width(first, size, unit):
    return 2 * unit if first % (2 * unit) == 0 and size % (2 * unit) == 0 else unit


def swap(count, distance):
    return [(t, t ^ distance) for t in range(count)]


def my_group():
    members = lax.axis_size("tile") // lax.axis_size("blk")
    return lax.axis_index("tile") // members


def token_spec():
    return pl.BlockSpec((16, LANES), lambda i: (0, 0))


def token_shape():
    return jax.ShapeDtypeStruct((16, LANES), jnp.bfloat16)


def as_columns(row, width):
    column = jnp.broadcast_to(row, (LANES, row.shape[1])).T
    return jnp.concatenate([column] * (width // LANES), axis=1)


def weigh_kernel(groups, *refs):
    sources, outs = refs[:6], refs[7 : 7 + groups]
    *held, weighted, sems = refs[7 + groups :]
    copies = [
        pltpu.make_async_copy(source, target, sems.at[i])
        for i, (source, target) in enumerate(zip(sources, held))
    ]
    for copy in copies:
        copy.start()
    for copy in copies:
        copy.wait()
    assign, orders, offsets, right, row_weight, coupling = held
    height, width = right.shape
    me = lax.axis_index("blk")
    right_wide = right[...].astype(jnp.float32)
    coupled = as_columns(coupling[...], width)
    scaled = coupled * right_wide
    row_ids = lax.broadcasted_iota(jnp.int32, (height, width), 0)
    live = jnp.zeros((height, width), jnp.float32)
    spread = jnp.zeros((height, width), jnp.float32)
    for b in range(assign.shape[0]):
        mine = assign[b] == me
        first = jnp.where(mine, offsets[b], 0)
        last = jnp.where(mine, offsets[b] + orders[b], 0)
        member = ((row_ids >= first) & (row_ids < last)).astype(jnp.float32)
        block_sum = jnp.sum(member * scaled, axis=0, keepdims=True)
        root = jnp.sqrt(jnp.full((1, width), orders[b], jnp.int32).astype(jnp.float32))
        spread += member * (block_sum / root)
        live += member
    result = live * as_columns(row_weight[...], width) * right_wide + coupled * spread
    weighted[...] = result.astype(jnp.bfloat16)
    group, rows = my_group(), outs[0].shape[0]
    for distance, out in enumerate(outs):
        start = pl.multiple_of(jnp.bitwise_xor(group, distance) * rows, rows)
        out[...] = weighted[pl.ds(start, rows), :]


def weigh_rows(right_rows, row_weight, coupling, assign, orders, offsets, after):
    height, width = right_rows.shape
    groups = lax.axis_size("blk")
    row_weight, coupling = row_weight.reshape(1, height), coupling.reshape(1, height)
    operands = (assign, orders, offsets, right_rows, row_weight, coupling)
    spaces = [pltpu.SMEM] * 3 + [pltpu.VMEM] * 3
    return pl.pallas_call(
        functools.partial(weigh_kernel, groups),
        grid=(1,),
        in_specs=[pl.BlockSpec(memory_space=pltpu.HBM)] * 6 + [token_spec()],
        out_specs=[pl.BlockSpec((height // groups, width), lambda i: (0, 0))] * groups,
        out_shape=[jax.ShapeDtypeStruct((height // groups, width), jnp.bfloat16)] * groups,
        scratch_shapes=[space(a.shape, a.dtype) for space, a in zip(spaces, operands)]
        + [pltpu.VMEM((height, width), jnp.bfloat16), pltpu.SemaphoreType.DMA((6,))],
        compiler_params=pltpu.CompilerParams(vmem_limit_bytes=VMEM_LIMIT),
        cost_estimate=cost(100000),
    )(*operands, after)


def pick_kernel(*refs):
    count = (len(refs) - 2) // 2
    pieces, outs, token, held = refs[:count], refs[count:-2], refs[-2], refs[-1]
    token[...] = jnp.zeros_like(token)
    for distance, piece in enumerate(pieces):
        held[distance] = piece[...]
    place = on_ring(lax.axis_index("blk"), count)
    group = my_group()
    for step, out in enumerate(outs):
        target = on_ring(lax.rem(place + step, count), count)
        out[...] = held[jnp.bitwise_xor(group, target)]


def pick_columns(pieces):
    count = len(pieces)
    return pl.pallas_call(
        pick_kernel,
        out_shape=[jax.ShapeDtypeStruct(pieces[0].shape, pieces[0].dtype)] * count
        + [token_shape()],
        scratch_shapes=[pltpu.VMEM((count, *pieces[0].shape), pieces[0].dtype)],
        compiler_params=pltpu.CompilerParams(vmem_limit_bytes=VMEM_LIMIT),
        cost_estimate=cost(1),
    )(*pieces)


def stack_kernel(*refs):
    parts, (_, out, token) = refs[:-3], refs[-3:]
    token[...] = jnp.zeros_like(token)
    for step, part in enumerate(parts):
        out[step] = part[...]


def whole_spec(shape):
    return pl.BlockSpec(tuple(shape), lambda i: (0,) * len(shape))


def stack_parts(parts, after, weight=1):
    shape = (len(parts), *parts[0].shape)
    return pl.pallas_call(
        stack_kernel,
        grid=(1,),
        in_specs=[whole_spec(part.shape) for part in parts] + [token_spec()],
        out_specs=[whole_spec(shape), token_spec()],
        out_shape=[jax.ShapeDtypeStruct(shape, parts[0].dtype), token_shape()],
        compiler_params=pltpu.CompilerParams(vmem_limit_bytes=VMEM_LIMIT),
        cost_estimate=cost(weight),
    )(*parts, after)


def arrange_kernel(places, members, *refs):
    pieces, (_, out, token, held) = refs[:-4], refs[-4:]
    token[...] = jnp.zeros_like(token)
    _, slabs, rows, width = pieces[0].shape
    height = held.shape[0] // slabs
    group, member = my_group(), lax.rem(lax.axis_index("tile"), members)
    for (far_member, far_groups), piece in zip(places, pieces):
        column = pl.multiple_of(jnp.bitwise_xor(member, far_member) * width, width)
        for index, far_group in enumerate(far_groups):
            row = pl.multiple_of(jnp.bitwise_xor(group, far_group) * rows, rows)
            for slab in range(slabs):
                held[pl.ds(slab * height + row, rows), pl.ds(column, width)] = piece[index, slab]
    for place, slab in enumerate(sorted(range(slabs), key=lambda s: (s == slabs // 2, s))):
        out[:, pl.ds(place * height, height)] = held[pl.ds(slab * height, height), :].T


def arrange(places, pieces, members, height, after):
    _, slabs, _, width = pieces[0].shape
    shape = (members * width, slabs * height)
    return pl.pallas_call(
        functools.partial(arrange_kernel, places, members),
        grid=(1,),
        in_specs=[whole_spec(piece.shape) for piece in pieces] + [token_spec()],
        out_specs=[whole_spec(shape), token_spec()],
        out_shape=[jax.ShapeDtypeStruct(shape, jnp.bfloat16), token_shape()],
        scratch_shapes=[pltpu.VMEM(shape[::-1], jnp.bfloat16)],
        compiler_params=pltpu.CompilerParams(vmem_limit_bytes=VMEM_LIMIT),
        cost_estimate=cost(1),
    )(*pieces, after)


def slice_kernel(left, *refs):
    out, token = refs[-2:]
    out[...] = left[...]
    token[...] = jnp.zeros_like(token)


def slice_columns(left_rows, first, size, unit, after):
    unit = block_width(first, size, unit)
    height, begin = left_rows.shape[0], first // unit
    return pl.pallas_call(
        slice_kernel,
        grid=(size // unit,),
        in_specs=[pl.BlockSpec((height, unit), lambda j: (0, begin + j))]
        + [token_spec()] * len(after),
        out_specs=[pl.BlockSpec((height, unit), lambda j: (0, j)), token_spec()],
        out_shape=[jax.ShapeDtypeStruct((height, size), left_rows.dtype), token_shape()],
        compiler_params=pltpu.CompilerParams(vmem_limit_bytes=VMEM_LIMIT),
        cost_estimate=cost(1),
    )(left_rows, *after)


def send_slab(piece):
    blks = lax.axis_size("blk")
    forth, back = ring_shift(blks, 1), ring_shift(blks, -1)
    ahead, behind = [], []
    for _ in range(blks // 2 - 1):
        ahead.append(lax.ppermute(ahead[-1] if ahead else piece, "blk", forth))
        behind.append(lax.ppermute(behind[-1] if behind else piece, "blk", back))
    return ahead, behind


def cut_kernel(ahead, behind, *refs):
    low, high, token = refs[-3:]
    low[...] = ahead[: low.shape[0], :]
    high[...] = behind[low.shape[0] :, :]
    token[...] = jnp.zeros_like(token)


def cut_far(ahead, behind, first, size, unit, shift, after):
    unit = size if first % size == 0 else block_width(first, size, unit)
    height, begin = ahead[-1].shape[0], first // unit
    low, high = height // 2 - shift, height // 2 + shift
    return pl.pallas_call(
        cut_kernel,
        grid=(size // unit,),
        in_specs=[pl.BlockSpec((height, unit), lambda j: (0, begin + j))] * 2
        + [token_spec()] * len(after),
        out_specs=[
            pl.BlockSpec((low, unit), lambda j: (0, j)),
            pl.BlockSpec((high, unit), lambda j: (0, j)),
            token_spec(),
        ],
        out_shape=[
            jax.ShapeDtypeStruct((low, size), ahead[-1].dtype),
            jax.ShapeDtypeStruct((high, size), ahead[-1].dtype),
            token_shape(),
        ],
        compiler_params=pltpu.CompilerParams(vmem_limit_bytes=VMEM_LIMIT),
        cost_estimate=cost(1),
    )(ahead[-1], behind[-1], *after)


def send_far(cuts):
    blks = lax.axis_size("blk")
    return [lax.ppermute(cut, "blk", ring_shift(blks, by)) for cut, by in zip(cuts, (1, -1))]


def stacked_dot(weights, pieces):
    stacked = jnp.concatenate([piece[...] for piece in pieces], axis=0)
    return jnp.dot(weights, stacked, preferred_element_type=jnp.float32)


def near_kernel(*refs):
    weights, pieces, (_, out, token) = refs[0], refs[1:-3], refs[-3:]
    token[...] = jnp.zeros_like(token)
    depth = sum(piece.shape[0] for piece in pieces)
    out[...] = stacked_dot(weights[:, :depth], pieces)


def far_kernel_onto(_, *refs):
    far_kernel(*refs)


def far_kernel(near, weights, *refs):
    pieces, (_, out, token) = refs[:-3], refs[-3:]
    token[...] = jnp.zeros_like(token)
    rows = out.shape[0]
    stacked = jnp.concatenate([piece[...] for piece in pieces], axis=0)
    last = pl.ds(weights.shape[1] - stacked.shape[0], stacked.shape[0])
    here = pl.ds(pl.multiple_of(pl.program_id(0) * rows, rows), rows)
    added = jnp.dot(weights[here, last], stacked, preferred_element_type=jnp.float32)
    out[...] = (near[here, :] + added).astype(out.dtype)


def piece_specs(pieces, unit):
    return [
        pl.BlockSpec((array.shape[0], unit), lambda j, begin=first // unit: (0, begin + j))
        for array, first in pieces
    ]


def near_chunk(weights, pieces, width, unit, after):
    rows, depth = weights.shape
    return pl.pallas_call(
        near_kernel,
        grid=(width // unit,),
        in_specs=[pl.BlockSpec((rows, depth), lambda j: (0, 0))]
        + piece_specs(pieces, unit)
        + [token_spec()],
        out_specs=[pl.BlockSpec((rows, unit), lambda j: (0, j)), token_spec()],
        out_shape=[jax.ShapeDtypeStruct((rows, width), jnp.float32), token_shape()],
        compiler_params=pltpu.CompilerParams(vmem_limit_bytes=VMEM_LIMIT),
        cost_estimate=cost(1),
    )(weights, *[array for array, _ in pieces], after)


def band_chunk(band, near, weights, pieces, begin, columns, after):
    rows, width = near.shape
    kernel, operands, specs, aliases = far_kernel, [], [], {}
    if band is not None:
        kernel, operands, aliases = far_kernel_onto, [band], {0: 0}
        specs = [pl.BlockSpec(memory_space=pl.ANY)]
    specs += [pl.BlockSpec(memory_space=pltpu.VMEM)] * 2
    steps, height = 2, rows // 2
    specs += [pl.BlockSpec(memory_space=pltpu.VMEM)] * len(pieces)
    out_spec = pl.BlockSpec(
        (pl.Element(height), pl.Element(width)), lambda i: (i * height, begin)
    )
    return pl.pallas_call(
        kernel,
        grid=(steps,),
        in_specs=specs + [token_spec()],
        out_specs=[out_spec, token_spec()],
        out_shape=[jax.ShapeDtypeStruct((rows, columns), jnp.bfloat16), token_shape()],
        input_output_aliases=aliases,
        compiler_params=pltpu.CompilerParams(vmem_limit_bytes=VMEM_LIMIT),
        cost_estimate=cost(1),
    )(*operands, near, weights, *pieces, after)


def shards(left_rows, right_rows, row_weight, coupling, assign, orders, offsets):
    height, columns = left_rows.shape
    blks, tiles = lax.axis_size("blk"), lax.axis_size("tile")
    members = tiles // blks
    unit = columns // UNITS

    starts = [sum(map(sum, SENDS[:i])) * unit for i in range(len(SENDS))]
    widths = [sum(sizes) * unit for sizes in SENDS]
    head = left_rows[:, : widths[0]]
    streams = [send_slab(head)]

    blocks = weigh_rows(right_rows, row_weight, coupling, assign, orders, offsets, head)
    pieces = [blocks[0]]
    for distance in range(1, blks):
        pieces.append(lax.ppermute(blocks[distance], "tile", swap(tiles, distance * members)))
    *parts, token = pick_columns(pieces)
    for step in range(1, blks):
        parts[step] = lax.ppermute(parts[step], "blk", ring_shift(blks, step))

    chunks = []

    def send_chunk(which, place, token, after=()):
        (ahead, behind), width = streams[which], SENDS[which][place] * unit
        offset = sum(SENDS[which][:place]) * unit
        *cuts, token = cut_far(
            ahead, behind, offset, width, unit, SHIFT[len(chunks)], [token, *after]
        )
        chunks.append((starts[which] + offset, send_far(cuts)))
        return token

    def send_slice(which, token, after=()):
        slab, token = slice_columns(left_rows, starts[which], widths[which], unit, [token, *after])
        streams.append(send_slab(slab))
        return token

    def multiply_near(which, place, token):
        (ahead, behind), offset = streams[which], sum(SENDS[which][:place]) * unit
        width, begin = SENDS[which][place] * unit, starts[which] + offset
        pieces = [(left_rows, begin)] + [(array, offset) for array in ahead + behind[::-1]]
        return near_chunk(weights, pieces, width, block_width(begin, width, unit), token)

    def multiply(band, near, index, token):
        begin, far = chunks[index]
        return band_chunk(band, near, weights, far, begin, columns, token)

    token = send_slice(1, token)
    token = send_chunk(0, 0, token)
    held, token = stack_parts(parts, token, 100000)
    held, far_groups = held[None], [0]
    bit = blks // 2
    while bit > 1:
        moved = lax.ppermute(held, "tile", swap(tiles, bit * members))
        held, token = stack_parts([held, moved], token)
        held = held.reshape((-1, *held.shape[2:]))
        far_groups = far_groups + [group ^ bit for group in far_groups]
        bit //= 2
    moved = lax.ppermute(held, "tile", swap(tiles, members))
    arrived = {(0, tuple(far_groups)): held, (0, tuple(g ^ 1 for g in far_groups)): moved}
    bit = members // 2
    while bit:
        for (member, groups), piece in list(arrived.items()):
            arrived[member ^ bit, groups] = lax.ppermute(piece, "tile", swap(tiles, bit))
        bit //= 2
    weights, token = arrange(
        list(arrived.keys()), list(arrived.values()), members, height, token
    )

    nears = [None] * sum(map(len, SENDS))
    nears[0], token = multiply_near(0, 0, token)
    token = send_slice(2, token, [streams[1][0][-1], streams[1][1][-1]])
    nears[1], token = multiply_near(1, 0, token)
    nears[2], token = multiply_near(1, 1, token)
    token = send_chunk(1, 0, token, chunks[0][-1])
    band, token = multiply(None, nears[0], 0, token)
    token = send_chunk(1, 1, token, [streams[2][0][-1], streams[2][1][-1]])
    nears[3], token = multiply_near(2, 0, token)
    token = send_chunk(2, 0, token, chunks[1][-1])
    for index in range(1, len(chunks)):
        band, token = multiply(band, nears[index], index, token)
    return band


def solution(mesh):
    return jax.shard_map(
        shards,
        mesh=mesh,
        in_specs=(P("blk", "tile"), P("blk", "tile"), P("blk"), P("blk"), P(), P(), P()),
        out_specs=P("blk", "tile"),
        check_vma=False,
    )
```

```python
import functools

import jax
import jax.numpy as jnp
from jax import lax
from jax.experimental import pallas as pl
from jax.experimental.pallas import tpu as pltpu
from jax.sharding import PartitionSpec as P

UNITS = 24
SENDS = ((8,), (6, 6), (4,))
SHIFT = (0, 16, 0, 0)
LANES = 128
VMEM_LIMIT = 16 * 1024 * 1024


def cost(weight):
    return pl.CostEstimate(flops=weight * 10**6, bytes_accessed=0, transcendentals=0)


def on_ring(place, count):
    half = count // 2
    return jnp.where(place < half, place, count + half - 1 - place)


def ring_shift(count, by):
    half = count // 2
    ring = list(range(half)) + list(range(count - 1, half - 1, -1))
    return [(ring[p], ring[(p + by) % count]) for p in range(count)]


def block_width(first, size, unit):
    return 2 * unit if first % (2 * unit) == 0 and size % (2 * unit) == 0 else unit


def swap(count, distance):
    return [(t, t ^ distance) for t in range(count)]


def my_group():
    members = lax.axis_size("tile") // lax.axis_size("blk")
    return lax.axis_index("tile") // members


def token_spec():
    return pl.BlockSpec((16, LANES), lambda i: (0, 0))


def token_shape():
    return jax.ShapeDtypeStruct((16, LANES), jnp.bfloat16)


def as_columns(row, width):
    column = jnp.broadcast_to(row, (LANES, row.shape[1])).T
    return jnp.concatenate([column] * (width // LANES), axis=1)


def weigh_kernel(groups, *refs):
    sources, outs = refs[:6], refs[7 : 7 + groups]
    *held, weighted, sems = refs[7 + groups :]
    copies = [
        pltpu.make_async_copy(source, target, sems.at[i])
        for i, (source, target) in enumerate(zip(sources, held))
    ]
    for copy in copies:
        copy.start()
    for copy in copies:
        copy.wait()
    assign, orders, offsets, right, row_weight, coupling = held
    height, width = right.shape
    me = lax.axis_index("blk")
    right_wide = right[...].astype(jnp.float32)
    coupled = as_columns(coupling[...], width)
    scaled = coupled * right_wide
    row_ids = lax.broadcasted_iota(jnp.int32, (height, width), 0)
    live = jnp.zeros((height, width), jnp.float32)
    spread = jnp.zeros((height, width), jnp.float32)
    for b in range(assign.shape[0]):
        mine = assign[b] == me
        first = jnp.where(mine, offsets[b], 0)
        last = jnp.where(mine, offsets[b] + orders[b], 0)
        member = ((row_ids >= first) & (row_ids < last)).astype(jnp.float32)
        block_sum = jnp.sum(member * scaled, axis=0, keepdims=True)
        root = jnp.sqrt(jnp.full((1, width), orders[b], jnp.int32).astype(jnp.float32))
        spread += member * (block_sum / root)
        live += member
    result = live * as_columns(row_weight[...], width) * right_wide + coupled * spread
    weighted[...] = result.astype(jnp.bfloat16)
    group, rows = my_group(), outs[0].shape[0]
    for distance, out in enumerate(outs):
        start = pl.multiple_of(jnp.bitwise_xor(group, distance) * rows, rows)
        out[...] = weighted[pl.ds(start, rows), :]


def weigh_rows(right_rows, row_weight, coupling, assign, orders, offsets, after):
    height, width = right_rows.shape
    groups = lax.axis_size("blk")
    row_weight, coupling = row_weight.reshape(1, height), coupling.reshape(1, height)
    operands = (assign, orders, offsets, right_rows, row_weight, coupling)
    spaces = [pltpu.SMEM] * 3 + [pltpu.VMEM] * 3
    return pl.pallas_call(
        functools.partial(weigh_kernel, groups),
        grid=(1,),
        in_specs=[pl.BlockSpec(memory_space=pltpu.HBM)] * 6 + [token_spec()],
        out_specs=[pl.BlockSpec((height // groups, width), lambda i: (0, 0))] * groups,
        out_shape=[jax.ShapeDtypeStruct((height // groups, width), jnp.bfloat16)] * groups,
        scratch_shapes=[space(a.shape, a.dtype) for space, a in zip(spaces, operands)]
        + [pltpu.VMEM((height, width), jnp.bfloat16), pltpu.SemaphoreType.DMA((6,))],
        compiler_params=pltpu.CompilerParams(vmem_limit_bytes=VMEM_LIMIT),
        cost_estimate=cost(100000),
    )(*operands, after)


def pick_kernel(*refs):
    count = (len(refs) - 2) // 2
    pieces, outs, token, held = refs[:count], refs[count:-2], refs[-2], refs[-1]
    token[...] = jnp.zeros_like(token)
    for distance, piece in enumerate(pieces):
        held[distance] = piece[...]
    place = on_ring(lax.axis_index("blk"), count)
    group = my_group()
    for step, out in enumerate(outs):
        target = on_ring(lax.rem(place + step, count), count)
        out[...] = held[jnp.bitwise_xor(group, target)]


def pick_columns(pieces):
    count = len(pieces)
    return pl.pallas_call(
        pick_kernel,
        out_shape=[jax.ShapeDtypeStruct(pieces[0].shape, pieces[0].dtype)] * count
        + [token_shape()],
        scratch_shapes=[pltpu.VMEM((count, *pieces[0].shape), pieces[0].dtype)],
        compiler_params=pltpu.CompilerParams(vmem_limit_bytes=VMEM_LIMIT),
        cost_estimate=cost(1),
    )(*pieces)


def stack_kernel(*refs):
    parts, (_, out, token) = refs[:-3], refs[-3:]
    token[...] = jnp.zeros_like(token)
    for step, part in enumerate(parts):
        out[step] = part[...]


def whole_spec(shape):
    return pl.BlockSpec(tuple(shape), lambda i: (0,) * len(shape))


def stack_parts(parts, after, weight=1):
    shape = (len(parts), *parts[0].shape)
    return pl.pallas_call(
        stack_kernel,
        grid=(1,),
        in_specs=[whole_spec(part.shape) for part in parts] + [token_spec()],
        out_specs=[whole_spec(shape), token_spec()],
        out_shape=[jax.ShapeDtypeStruct(shape, parts[0].dtype), token_shape()],
        compiler_params=pltpu.CompilerParams(vmem_limit_bytes=VMEM_LIMIT),
        cost_estimate=cost(weight),
    )(*parts, after)


def arrange_kernel(places, members, *refs):
    pieces, (_, out, token, held) = refs[:-4], refs[-4:]
    token[...] = jnp.zeros_like(token)
    _, slabs, rows, width = pieces[0].shape
    height = held.shape[0] // slabs
    group, member = my_group(), lax.rem(lax.axis_index("tile"), members)
    for (far_member, far_groups), piece in zip(places, pieces):
        column = pl.multiple_of(jnp.bitwise_xor(member, far_member) * width, width)
        for index, far_group in enumerate(far_groups):
            row = pl.multiple_of(jnp.bitwise_xor(group, far_group) * rows, rows)
            for slab in range(slabs):
                held[pl.ds(slab * height + row, rows), pl.ds(column, width)] = piece[index, slab]
    for place, slab in enumerate(sorted(range(slabs), key=lambda s: (s == slabs // 2, s))):
        out[:, pl.ds(place * height, height)] = held[pl.ds(slab * height, height), :].T


def arrange(places, pieces, members, height, after):
    _, slabs, _, width = pieces[0].shape
    shape = (members * width, slabs * height)
    return pl.pallas_call(
        functools.partial(arrange_kernel, places, members),
        grid=(1,),
        in_specs=[whole_spec(piece.shape) for piece in pieces] + [token_spec()],
        out_specs=[whole_spec(shape), token_spec()],
        out_shape=[jax.ShapeDtypeStruct(shape, jnp.bfloat16), token_shape()],
        scratch_shapes=[pltpu.VMEM(shape[::-1], jnp.bfloat16)],
        compiler_params=pltpu.CompilerParams(vmem_limit_bytes=VMEM_LIMIT),
        cost_estimate=cost(1),
    )(*pieces, after)


def slice_kernel(left, *refs):
    out, token = refs[-2:]
    out[...] = left[...]
    token[...] = jnp.zeros_like(token)


def slice_columns(left_rows, first, size, unit, after):
    unit = block_width(first, size, unit)
    height, begin = left_rows.shape[0], first // unit
    return pl.pallas_call(
        slice_kernel,
        grid=(size // unit,),
        in_specs=[pl.BlockSpec((height, unit), lambda j: (0, begin + j))]
        + [token_spec()] * len(after),
        out_specs=[pl.BlockSpec((height, unit), lambda j: (0, j)), token_spec()],
        out_shape=[jax.ShapeDtypeStruct((height, size), left_rows.dtype), token_shape()],
        compiler_params=pltpu.CompilerParams(vmem_limit_bytes=VMEM_LIMIT),
        cost_estimate=cost(1),
    )(left_rows, *after)


def send_slab(piece):
    blks = lax.axis_size("blk")
    forth, back = ring_shift(blks, 1), ring_shift(blks, -1)
    ahead, behind = [], []
    for _ in range(blks // 2 - 1):
        ahead.append(lax.ppermute(ahead[-1] if ahead else piece, "blk", forth))
        behind.append(lax.ppermute(behind[-1] if behind else piece, "blk", back))
    return ahead, behind


def cut_kernel(ahead, behind, *refs):
    low, high, token = refs[-3:]
    low[...] = ahead[: low.shape[0], :]
    high[...] = behind[low.shape[0] :, :]
    token[...] = jnp.zeros_like(token)


def cut_far(ahead, behind, first, size, unit, shift, after):
    unit = size if first % size == 0 else block_width(first, size, unit)
    height, begin = ahead[-1].shape[0], first // unit
    low, high = height // 2 - shift, height // 2 + shift
    return pl.pallas_call(
        cut_kernel,
        grid=(size // unit,),
        in_specs=[pl.BlockSpec((height, unit), lambda j: (0, begin + j))] * 2
        + [token_spec()] * len(after),
        out_specs=[
            pl.BlockSpec((low, unit), lambda j: (0, j)),
            pl.BlockSpec((high, unit), lambda j: (0, j)),
            token_spec(),
        ],
        out_shape=[
            jax.ShapeDtypeStruct((low, size), ahead[-1].dtype),
            jax.ShapeDtypeStruct((high, size), ahead[-1].dtype),
            token_shape(),
        ],
        compiler_params=pltpu.CompilerParams(vmem_limit_bytes=VMEM_LIMIT),
        cost_estimate=cost(1),
    )(ahead[-1], behind[-1], *after)


def send_far(cuts):
    blks = lax.axis_size("blk")
    return [lax.ppermute(cut, "blk", ring_shift(blks, by)) for cut, by in zip(cuts, (1, -1))]


def stacked_dot(weights, pieces):
    stacked = jnp.concatenate([piece[...] for piece in pieces], axis=0)
    return jnp.dot(weights, stacked, preferred_element_type=jnp.float32)


def near_kernel(*refs):
    weights, pieces, (_, out, token) = refs[0], refs[1:-3], refs[-3:]
    token[...] = jnp.zeros_like(token)
    depth = sum(piece.shape[0] for piece in pieces)
    out[...] = stacked_dot(weights[:, :depth], pieces)


def far_kernel_onto(_, *refs):
    far_kernel(*refs)


def far_kernel(near, weights, *refs):
    if len(refs) == 3:
        *pieces, out = refs
    else:
        *pieces, _, out, token = refs
        token[...] = jnp.zeros_like(token)
    rows = out.shape[0]
    stacked = jnp.concatenate([piece[...] for piece in pieces], axis=0)
    last = pl.ds(weights.shape[1] - stacked.shape[0], stacked.shape[0])
    here = pl.ds(pl.multiple_of(pl.program_id(0) * rows, rows), rows)
    added = jnp.dot(weights[here, last], stacked, preferred_element_type=jnp.float32)
    out[...] = (near[here, :] + added).astype(out.dtype)


def piece_specs(pieces, unit):
    return [
        pl.BlockSpec((array.shape[0], unit), lambda j, begin=first // unit: (0, begin + j))
        for array, first in pieces
    ]


def near_chunk(weights, pieces, width, unit, after):
    rows, depth = weights.shape
    return pl.pallas_call(
        near_kernel,
        grid=(width // unit,),
        in_specs=[pl.BlockSpec((rows, depth), lambda j: (0, 0))]
        + piece_specs(pieces, unit)
        + [token_spec()],
        out_specs=[pl.BlockSpec((rows, unit), lambda j: (0, j)), token_spec()],
        out_shape=[jax.ShapeDtypeStruct((rows, width), jnp.float32), token_shape()],
        compiler_params=pltpu.CompilerParams(vmem_limit_bytes=VMEM_LIMIT),
        cost_estimate=cost(1),
    )(weights, *[array for array, _ in pieces], after)


def band_chunk(band, near, weights, pieces, begin, columns, after):
    rows, width = near.shape
    kernel, operands, specs, aliases = far_kernel, [], [], {}
    if band is not None:
        kernel, operands, aliases = far_kernel_onto, [band], {0: 0}
        specs = [pl.BlockSpec(memory_space=pl.ANY)]
    specs += [pl.BlockSpec(memory_space=pltpu.VMEM)] * 2
    steps, height = 2, rows // 2
    specs += [pl.BlockSpec(memory_space=pltpu.VMEM)] * len(pieces)
    out_spec = pl.BlockSpec(
        (pl.Element(height), pl.Element(width)), lambda i: (i * height, begin)
    )
    return pl.pallas_call(
        kernel,
        grid=(steps,),
        in_specs=specs + [token_spec()] * len(after),
        out_specs=[out_spec] + [token_spec()] * len(after),
        out_shape=[jax.ShapeDtypeStruct((rows, columns), jnp.bfloat16)]
        + [token_shape()] * len(after),
        input_output_aliases=aliases,
        compiler_params=pltpu.CompilerParams(vmem_limit_bytes=VMEM_LIMIT),
        cost_estimate=cost(1),
    )(*operands, near, weights, *pieces, *after)


def shards(left_rows, right_rows, row_weight, coupling, assign, orders, offsets):
    height, columns = left_rows.shape
    blks, tiles = lax.axis_size("blk"), lax.axis_size("tile")
    members = tiles // blks
    unit = columns // UNITS

    starts = [sum(map(sum, SENDS[:i])) * unit for i in range(len(SENDS))]
    widths = [sum(sizes) * unit for sizes in SENDS]
    head = left_rows[:, : widths[0]]
    streams = [send_slab(head)]

    blocks = weigh_rows(right_rows, row_weight, coupling, assign, orders, offsets, head)
    pieces = [blocks[0]]
    for distance in range(1, blks):
        pieces.append(lax.ppermute(blocks[distance], "tile", swap(tiles, distance * members)))
    *parts, token = pick_columns(pieces)
    for step in range(1, blks):
        parts[step] = lax.ppermute(parts[step], "blk", ring_shift(blks, step))

    chunks = []

    def send_chunk(which, place, token, after=()):
        (ahead, behind), width = streams[which], SENDS[which][place] * unit
        offset = sum(SENDS[which][:place]) * unit
        *cuts, token = cut_far(
            ahead, behind, offset, width, unit, SHIFT[len(chunks)], [token, *after]
        )
        chunks.append((starts[which] + offset, send_far(cuts)))
        return token

    def send_slice(which, token, after=()):
        slab, token = slice_columns(left_rows, starts[which], widths[which], unit, [token, *after])
        streams.append(send_slab(slab))
        return token

    def multiply_near(which, place, token):
        (ahead, behind), offset = streams[which], sum(SENDS[which][:place]) * unit
        width, begin = SENDS[which][place] * unit, starts[which] + offset
        pieces = [(left_rows, begin)] + [(array, offset) for array in ahead + behind[::-1]]
        return near_chunk(weights, pieces, width, block_width(begin, width, unit), token)

    def multiply(band, near, index, after):
        begin, far = chunks[index]
        return band_chunk(band, near, weights, far, begin, columns, after)

    token = send_slice(1, token)
    token = send_chunk(0, 0, token)
    held, token = stack_parts(parts, token, 100000)
    held, far_groups = held[None], [0]
    bit = blks // 2
    while bit > 1:
        moved = lax.ppermute(held, "tile", swap(tiles, bit * members))
        held, token = stack_parts([held, moved], token)
        held = held.reshape((-1, *held.shape[2:]))
        far_groups = far_groups + [group ^ bit for group in far_groups]
        bit //= 2
    moved = lax.ppermute(held, "tile", swap(tiles, members))
    arrived = {(0, tuple(far_groups)): held, (0, tuple(g ^ 1 for g in far_groups)): moved}
    bit = members // 2
    while bit:
        for (member, groups), piece in list(arrived.items()):
            arrived[member ^ bit, groups] = lax.ppermute(piece, "tile", swap(tiles, bit))
        bit //= 2
    weights, token = arrange(
        list(arrived.keys()), list(arrived.values()), members, height, token
    )

    nears = [None] * sum(map(len, SENDS))
    nears[0], token = multiply_near(0, 0, token)
    token = send_slice(2, token, [streams[1][0][-1], streams[1][1][-1]])
    nears[1], token = multiply_near(1, 0, token)
    nears[2], token = multiply_near(1, 1, token)
    token = send_chunk(1, 0, token, chunks[0][-1])
    band, token = multiply(None, nears[0], 0, [token])
    token = send_chunk(1, 1, token, [streams[2][0][-1], streams[2][1][-1]])
    nears[3], token = multiply_near(2, 0, token)
    token = send_chunk(2, 0, token, chunks[1][-1])
    band, _ = multiply(band, nears[1], 1, [token])
    for index in range(2, len(chunks)):
        (band,) = multiply(band, nears[index], index, [])
    return band


def solution(mesh):
    return jax.shard_map(
        shards,
        mesh=mesh,
        in_specs=(P("blk", "tile"), P("blk", "tile"), P("blk"), P("blk"), P(), P(), P()),
        out_specs=P("blk", "tile"),
        check_vma=False,
    )
```

```python
import functools

import jax
import jax.numpy as jnp
from jax import lax
from jax.experimental import pallas as pl
from jax.experimental.pallas import tpu as pltpu
from jax.sharding import PartitionSpec as P

UNITS = 24
SENDS = ((8,), (7, 5), (4,))
SHIFT = (0, 16, 0, 0)
LANES = 128
VMEM_LIMIT = 16 * 1024 * 1024


def cost(weight):
    return pl.CostEstimate(flops=weight * 10**6, bytes_accessed=0, transcendentals=0)


def on_ring(place, count):
    half = count // 2
    return jnp.where(place < half, place, count + half - 1 - place)


def ring_shift(count, by):
    half = count // 2
    ring = list(range(half)) + list(range(count - 1, half - 1, -1))
    return [(ring[p], ring[(p + by) % count]) for p in range(count)]


def block_width(first, size, unit):
    return 2 * unit if first % (2 * unit) == 0 and size % (2 * unit) == 0 else unit


def swap(count, distance):
    return [(t, t ^ distance) for t in range(count)]


def my_group():
    members = lax.axis_size("tile") // lax.axis_size("blk")
    return lax.axis_index("tile") // members


def token_spec():
    return pl.BlockSpec((16, LANES), lambda i: (0, 0))


def token_shape():
    return jax.ShapeDtypeStruct((16, LANES), jnp.bfloat16)


def as_columns(row, width):
    column = jnp.broadcast_to(row, (LANES, row.shape[1])).T
    return jnp.concatenate([column] * (width // LANES), axis=1)


def weigh_kernel(groups, *refs):
    sources, outs = refs[:6], refs[7 : 7 + groups]
    *held, weighted, sems = refs[7 + groups :]
    copies = [
        pltpu.make_async_copy(source, target, sems.at[i])
        for i, (source, target) in enumerate(zip(sources, held))
    ]
    for copy in copies:
        copy.start()
    for copy in copies:
        copy.wait()
    assign, orders, offsets, right, row_weight, coupling = held
    height, width = right.shape
    me = lax.axis_index("blk")
    right_wide = right[...].astype(jnp.float32)
    coupled = as_columns(coupling[...], width)
    scaled = coupled * right_wide
    row_ids = lax.broadcasted_iota(jnp.int32, (height, width), 0)
    live = jnp.zeros((height, width), jnp.float32)
    spread = jnp.zeros((height, width), jnp.float32)
    for b in range(assign.shape[0]):
        mine = assign[b] == me
        first = jnp.where(mine, offsets[b], 0)
        last = jnp.where(mine, offsets[b] + orders[b], 0)
        member = ((row_ids >= first) & (row_ids < last)).astype(jnp.float32)
        block_sum = jnp.sum(member * scaled, axis=0, keepdims=True)
        root = jnp.sqrt(jnp.full((1, width), orders[b], jnp.int32).astype(jnp.float32))
        spread += member * (block_sum / root)
        live += member
    result = live * as_columns(row_weight[...], width) * right_wide + coupled * spread
    weighted[...] = result.astype(jnp.bfloat16)
    group, rows = my_group(), outs[0].shape[0]
    for distance, out in enumerate(outs):
        start = pl.multiple_of(jnp.bitwise_xor(group, distance) * rows, rows)
        out[...] = weighted[pl.ds(start, rows), :]


def weigh_rows(right_rows, row_weight, coupling, assign, orders, offsets, after):
    height, width = right_rows.shape
    groups = lax.axis_size("blk")
    row_weight, coupling = row_weight.reshape(1, height), coupling.reshape(1, height)
    operands = (assign, orders, offsets, right_rows, row_weight, coupling)
    spaces = [pltpu.SMEM] * 3 + [pltpu.VMEM] * 3
    return pl.pallas_call(
        functools.partial(weigh_kernel, groups),
        grid=(1,),
        in_specs=[pl.BlockSpec(memory_space=pltpu.HBM)] * 6 + [token_spec()],
        out_specs=[pl.BlockSpec((height // groups, width), lambda i: (0, 0))] * groups,
        out_shape=[jax.ShapeDtypeStruct((height // groups, width), jnp.bfloat16)] * groups,
        scratch_shapes=[space(a.shape, a.dtype) for space, a in zip(spaces, operands)]
        + [pltpu.VMEM((height, width), jnp.bfloat16), pltpu.SemaphoreType.DMA((6,))],
        compiler_params=pltpu.CompilerParams(vmem_limit_bytes=VMEM_LIMIT),
        cost_estimate=cost(100000),
    )(*operands, after)


def pick_kernel(*refs):
    count = (len(refs) - 2) // 2
    pieces, outs, token, held = refs[:count], refs[count:-2], refs[-2], refs[-1]
    token[...] = jnp.zeros_like(token)
    for distance, piece in enumerate(pieces):
        held[distance] = piece[...]
    place = on_ring(lax.axis_index("blk"), count)
    group = my_group()
    for step, out in enumerate(outs):
        target = on_ring(lax.rem(place + step, count), count)
        out[...] = held[jnp.bitwise_xor(group, target)]


def pick_columns(pieces):
    count = len(pieces)
    return pl.pallas_call(
        pick_kernel,
        out_shape=[jax.ShapeDtypeStruct(pieces[0].shape, pieces[0].dtype)] * count
        + [token_shape()],
        scratch_shapes=[pltpu.VMEM((count, *pieces[0].shape), pieces[0].dtype)],
        compiler_params=pltpu.CompilerParams(vmem_limit_bytes=VMEM_LIMIT),
        cost_estimate=cost(1),
    )(*pieces)


def stack_kernel(*refs):
    parts, (_, out, token) = refs[:-3], refs[-3:]
    token[...] = jnp.zeros_like(token)
    for step, part in enumerate(parts):
        out[step] = part[...]


def whole_spec(shape):
    return pl.BlockSpec(tuple(shape), lambda i: (0,) * len(shape))


def stack_parts(parts, after, weight=1):
    shape = (len(parts), *parts[0].shape)
    return pl.pallas_call(
        stack_kernel,
        grid=(1,),
        in_specs=[whole_spec(part.shape) for part in parts] + [token_spec()],
        out_specs=[whole_spec(shape), token_spec()],
        out_shape=[jax.ShapeDtypeStruct(shape, parts[0].dtype), token_shape()],
        compiler_params=pltpu.CompilerParams(vmem_limit_bytes=VMEM_LIMIT),
        cost_estimate=cost(weight),
    )(*parts, after)


def arrange_kernel(places, members, *refs):
    pieces, (_, out, token, held) = refs[:-4], refs[-4:]
    token[...] = jnp.zeros_like(token)
    _, slabs, rows, width = pieces[0].shape
    height = held.shape[0] // slabs
    group, member = my_group(), lax.rem(lax.axis_index("tile"), members)
    for (far_member, far_groups), piece in zip(places, pieces):
        column = pl.multiple_of(jnp.bitwise_xor(member, far_member) * width, width)
        for index, far_group in enumerate(far_groups):
            row = pl.multiple_of(jnp.bitwise_xor(group, far_group) * rows, rows)
            for slab in range(slabs):
                held[pl.ds(slab * height + row, rows), pl.ds(column, width)] = piece[index, slab]
    for place, slab in enumerate(sorted(range(slabs), key=lambda s: (s == slabs // 2, s))):
        out[:, pl.ds(place * height, height)] = held[pl.ds(slab * height, height), :].T


def arrange(places, pieces, members, height, after):
    _, slabs, _, width = pieces[0].shape
    shape = (members * width, slabs * height)
    return pl.pallas_call(
        functools.partial(arrange_kernel, places, members),
        grid=(1,),
        in_specs=[whole_spec(piece.shape) for piece in pieces] + [token_spec()],
        out_specs=[whole_spec(shape), token_spec()],
        out_shape=[jax.ShapeDtypeStruct(shape, jnp.bfloat16), token_shape()],
        scratch_shapes=[pltpu.VMEM(shape[::-1], jnp.bfloat16)],
        compiler_params=pltpu.CompilerParams(vmem_limit_bytes=VMEM_LIMIT),
        cost_estimate=cost(1),
    )(*pieces, after)


def slice_kernel(left, *refs):
    out, token = refs[-2:]
    out[...] = left[...]
    token[...] = jnp.zeros_like(token)


def slice_columns(left_rows, first, size, unit, after):
    unit = block_width(first, size, unit)
    height, begin = left_rows.shape[0], first // unit
    return pl.pallas_call(
        slice_kernel,
        grid=(size // unit,),
        in_specs=[pl.BlockSpec((height, unit), lambda j: (0, begin + j))]
        + [token_spec()] * len(after),
        out_specs=[pl.BlockSpec((height, unit), lambda j: (0, j)), token_spec()],
        out_shape=[jax.ShapeDtypeStruct((height, size), left_rows.dtype), token_shape()],
        compiler_params=pltpu.CompilerParams(vmem_limit_bytes=VMEM_LIMIT),
        cost_estimate=cost(1),
    )(left_rows, *after)


def send_slab(piece):
    blks = lax.axis_size("blk")
    forth, back = ring_shift(blks, 1), ring_shift(blks, -1)
    ahead, behind = [], []
    for _ in range(blks // 2 - 1):
        ahead.append(lax.ppermute(ahead[-1] if ahead else piece, "blk", forth))
        behind.append(lax.ppermute(behind[-1] if behind else piece, "blk", back))
    return ahead, behind


def cut_kernel(ahead, behind, *refs):
    low, high, token = refs[-3:]
    low[...] = ahead[: low.shape[0], :]
    high[...] = behind[low.shape[0] :, :]
    token[...] = jnp.zeros_like(token)


def cut_far(ahead, behind, first, size, unit, shift, after):
    unit = size if first % size == 0 else block_width(first, size, unit)
    height, begin = ahead[-1].shape[0], first // unit
    low, high = height // 2 - shift, height // 2 + shift
    return pl.pallas_call(
        cut_kernel,
        grid=(size // unit,),
        in_specs=[pl.BlockSpec((height, unit), lambda j: (0, begin + j))] * 2
        + [token_spec()] * len(after),
        out_specs=[
            pl.BlockSpec((low, unit), lambda j: (0, j)),
            pl.BlockSpec((high, unit), lambda j: (0, j)),
            token_spec(),
        ],
        out_shape=[
            jax.ShapeDtypeStruct((low, size), ahead[-1].dtype),
            jax.ShapeDtypeStruct((high, size), ahead[-1].dtype),
            token_shape(),
        ],
        compiler_params=pltpu.CompilerParams(vmem_limit_bytes=VMEM_LIMIT),
        cost_estimate=cost(1),
    )(ahead[-1], behind[-1], *after)


def send_far(cuts):
    blks = lax.axis_size("blk")
    return [lax.ppermute(cut, "blk", ring_shift(blks, by)) for cut, by in zip(cuts, (1, -1))]


def stacked_dot(weights, pieces):
    stacked = jnp.concatenate([piece[...] for piece in pieces], axis=0)
    return jnp.dot(weights, stacked, preferred_element_type=jnp.float32)


def near_kernel(*refs):
    weights, pieces, (_, out, token) = refs[0], refs[1:-3], refs[-3:]
    token[...] = jnp.zeros_like(token)
    depth = sum(piece.shape[0] for piece in pieces)
    out[...] = stacked_dot(weights[:, :depth], pieces)


def far_kernel_onto(_, *refs):
    far_kernel(*refs)


def far_kernel(near, weights, *refs):
    pieces, (_, out, token) = refs[:-3], refs[-3:]
    token[...] = jnp.zeros_like(token)
    rows = out.shape[0]
    stacked = jnp.concatenate([piece[...] for piece in pieces], axis=0)
    last = pl.ds(weights.shape[1] - stacked.shape[0], stacked.shape[0])
    here = pl.ds(pl.multiple_of(pl.program_id(0) * rows, rows), rows)
    added = jnp.dot(weights[here, last], stacked, preferred_element_type=jnp.float32)
    out[...] = (near[here, :] + added).astype(out.dtype)


def piece_specs(pieces, unit):
    return [
        pl.BlockSpec((array.shape[0], unit), lambda j, begin=first // unit: (0, begin + j))
        for array, first in pieces
    ]


def near_chunk(weights, pieces, width, unit, after):
    rows, depth = weights.shape
    return pl.pallas_call(
        near_kernel,
        grid=(width // unit,),
        in_specs=[pl.BlockSpec((rows, depth), lambda j: (0, 0))]
        + piece_specs(pieces, unit)
        + [token_spec()],
        out_specs=[pl.BlockSpec((rows, unit), lambda j: (0, j)), token_spec()],
        out_shape=[jax.ShapeDtypeStruct((rows, width), jnp.float32), token_shape()],
        compiler_params=pltpu.CompilerParams(vmem_limit_bytes=VMEM_LIMIT),
        cost_estimate=cost(1),
    )(weights, *[array for array, _ in pieces], after)


def band_chunk(band, near, weights, pieces, begin, columns, after):
    rows, width = near.shape
    kernel, operands, specs, aliases = far_kernel, [], [], {}
    if band is not None:
        kernel, operands, aliases = far_kernel_onto, [band], {0: 0}
        specs = [pl.BlockSpec(memory_space=pl.ANY)]
    specs += [pl.BlockSpec(memory_space=pltpu.VMEM)] * 2
    steps, height = 2, rows // 2
    specs += [pl.BlockSpec(memory_space=pltpu.VMEM)] * len(pieces)
    out_spec = pl.BlockSpec(
        (pl.Element(height), pl.Element(width)), lambda i: (i * height, begin)
    )
    return pl.pallas_call(
        kernel,
        grid=(steps,),
        in_specs=specs + [token_spec()],
        out_specs=[out_spec, token_spec()],
        out_shape=[jax.ShapeDtypeStruct((rows, columns), jnp.bfloat16), token_shape()],
        input_output_aliases=aliases,
        compiler_params=pltpu.CompilerParams(vmem_limit_bytes=VMEM_LIMIT),
        cost_estimate=cost(1),
    )(*operands, near, weights, *pieces, after)


def shards(left_rows, right_rows, row_weight, coupling, assign, orders, offsets):
    height, columns = left_rows.shape
    blks, tiles = lax.axis_size("blk"), lax.axis_size("tile")
    members = tiles // blks
    unit = columns // UNITS

    starts = [sum(map(sum, SENDS[:i])) * unit for i in range(len(SENDS))]
    widths = [sum(sizes) * unit for sizes in SENDS]
    head = left_rows[:, : widths[0]]
    streams = [send_slab(head)]

    blocks = weigh_rows(right_rows, row_weight, coupling, assign, orders, offsets, head)
    pieces = [blocks[0]]
    for distance in range(1, blks):
        pieces.append(lax.ppermute(blocks[distance], "tile", swap(tiles, distance * members)))
    *parts, token = pick_columns(pieces)
    for step in range(1, blks):
        parts[step] = lax.ppermute(parts[step], "blk", ring_shift(blks, step))

    chunks = []

    def send_chunk(which, place, token, after=()):
        (ahead, behind), width = streams[which], SENDS[which][place] * unit
        offset = sum(SENDS[which][:place]) * unit
        *cuts, token = cut_far(
            ahead, behind, offset, width, unit, SHIFT[len(chunks)], [token, *after]
        )
        chunks.append((starts[which] + offset, send_far(cuts)))
        return token

    def send_slice(which, token, after=()):
        slab, token = slice_columns(left_rows, starts[which], widths[which], unit, [token, *after])
        streams.append(send_slab(slab))
        return token

    def multiply_near(which, place, token):
        (ahead, behind), offset = streams[which], sum(SENDS[which][:place]) * unit
        width, begin = SENDS[which][place] * unit, starts[which] + offset
        pieces = [(left_rows, begin)] + [(array, offset) for array in ahead + behind[::-1]]
        return near_chunk(weights, pieces, width, block_width(begin, width, unit), token)

    def multiply(band, near, index, token):
        begin, far = chunks[index]
        return band_chunk(band, near, weights, far, begin, columns, token)

    token = send_slice(1, token)
    token = send_chunk(0, 0, token)
    held, token = stack_parts(parts, token, 100000)
    held, far_groups = held[None], [0]
    bit = blks // 2
    while bit > 1:
        moved = lax.ppermute(held, "tile", swap(tiles, bit * members))
        held, token = stack_parts([held, moved], token)
        held = held.reshape((-1, *held.shape[2:]))
        far_groups = far_groups + [group ^ bit for group in far_groups]
        bit //= 2
    moved = lax.ppermute(held, "tile", swap(tiles, members))
    arrived = {(0, tuple(far_groups)): held, (0, tuple(g ^ 1 for g in far_groups)): moved}
    bit = members // 2
    while bit:
        for (member, groups), piece in list(arrived.items()):
            arrived[member ^ bit, groups] = lax.ppermute(piece, "tile", swap(tiles, bit))
        bit //= 2
    weights, token = arrange(
        list(arrived.keys()), list(arrived.values()), members, height, token
    )

    nears = [None] * sum(map(len, SENDS))
    nears[0], token = multiply_near(0, 0, token)
    token = send_slice(2, token, [streams[1][0][-1], streams[1][1][-1]])
    nears[1], token = multiply_near(1, 0, token)
    nears[2], token = multiply_near(1, 1, token)
    token = send_chunk(1, 0, token, chunks[0][-1])
    band, token = multiply(None, nears[0], 0, token)
    token = send_chunk(1, 1, token, [streams[2][0][-1], streams[2][1][-1]])
    nears[3], token = multiply_near(2, 0, token)
    token = send_chunk(2, 0, token, chunks[1][-1])
    for index in range(1, len(chunks)):
        band, token = multiply(band, nears[index], index, token)
    return band


def solution(mesh):
    return jax.shard_map(
        shards,
        mesh=mesh,
        in_specs=(P("blk", "tile"), P("blk", "tile"), P("blk"), P("blk"), P(), P(), P()),
        out_specs=P("blk", "tile"),
        check_vma=False,
    )
```
